32 devices in a mesh: dp: 4 (over x, core), expert: 8 (over z, y).
Axes of the slice: x: 2, y: 2, z: 4, core: 2. Of those that a mesh axis runs over, the one named last changes fastest.
Arguments:
- tokens: bfloat16 [4096, 4096], P(('dp', 'expert')), may hold values from -6 to 6
- output_gradient: bfloat16 [4096, 4096], P(('dp', 'expert')), may hold values from -6 to 6
- slot: int32 [4096, 1], P(('dp', 'expert')), may hold values from -1 to 7, as said below
- gate_weight: float32 [4096, 1], P(('dp', 'expert')), may hold values from 0.2 to 1
- gate_up_weight: bfloat16 [8, 4096, 384], P('expert', 'dp'), may hold values from -0.09375 to 0.09375
- down_weight: bfloat16 [8, 192, 4096], P('expert', None, 'dp'), may hold values from -0.15625 to 0.15625
Outputs:
- grad_tokens: bfloat16 [4096, 4096], P(('dp', 'expert'))
- grad_gate_up: bfloat16 [8, 4096, 384], P('expert', 'dp')
The draws below stay inside these ranges and needn't reach their ends.
Inputs may be any that keep to these rules, and one draw needn't show every extreme that they name: `slot`: within the tokens of one block of 128 and one window expert, the values other than -1 are 0, 1, ..., k - 1, each once; one window expert, the same one in every block, takes all 8 slots in every block, and each of the other window experts takes at most 4 slots in that block.
All inputs are finite; a program needn't handle non-finite values.
Results may differ from the reference program's by a relative error of at most 0.022.
Values may be sent and summed in bfloat16 or wider, within the bound.
A program may use at most 64 MiB of HBM per device.

```python
import jax
import jax.numpy as jnp
from jax import lax

D = 4096
F = 1536
GROUP = 8
TOK_DEV = 128
F_DEV = 192
CAP = 8
EXP_WIN = 1
TOKENS = 4096
N_DP = 4
N_EXPERT = 8


def draw_slot(key, part):
    blocks = TOKENS // TOK_DEV
    hot = jax.random.randint(jax.random.fold_in(key, 7), (), 0, EXP_WIN)
    keys = jax.random.split(jax.random.fold_in(key, 11), blocks * EXP_WIN)

    def one_list(sub_key, index):
        expert = index % EXP_WIN
        count_key, order_key = jax.random.split(sub_key)
        count = jax.random.randint(count_key, (), 1, CAP // 2 + 1)
        count = jnp.where(expert == hot, CAP, count)
        order = jax.random.permutation(order_key, TOK_DEV)
        ranks = jnp.argsort(order)
        return jnp.where(ranks < count, ranks, -1).astype(jnp.int32)
    lists = jax.vmap(one_list)(keys, jnp.arange(blocks * EXP_WIN, dtype=jnp.int32))
    return jnp.transpose(lists.reshape(blocks, EXP_WIN, TOK_DEV), (0, 2, 1)).reshape(TOKENS, EXP_WIN)


def levels(own_key, dims, cuts, smallest, high):
    factor_of = 1.0
    for dim, parts in cuts:
        heights = jax.random.uniform(jax.random.fold_in(jax.random.fold_in(own_key, 6), dim), (parts,), jnp.float32, smallest / len(cuts), high / len(cuts))
        factor_of = factor_of * jnp.repeat(jnp.exp(heights), dims[dim] // parts).reshape((-1,) + (1,) * (len(dims) - 1 - dim))
    return factor_of


def normal_values(key, dims, scale, most, cuts=(), kind=jnp.bfloat16):
    array = jax.random.normal(key, dims, jnp.float32) * scale
    if len(cuts) > 0:
        array = levels(key, dims, cuts, -0.22, 0.18) * array
    return jnp.clip(array, min=-most, max=most).astype(kind)


def setup_inputs(seed: int = 0) -> dict:
    key_of = jax.random.split(jax.random.key(seed), 7)
    tokens = normal_values(key_of[0], (TOKENS, D), 1.0, 6.0, ((0, 32),))
    output_gradient = normal_values(key_of[1], (TOKENS, D), 1.0, 6.0, ((0, 32),))
    slot = draw_slot(jax.random.fold_in(key_of[6], 71), 0)
    gate_weight = jnp.clip(0.2 + 0.8 * jax.random.uniform(key_of[3], (TOKENS, EXP_WIN), jnp.float32) ** levels(key_of[3], (TOKENS, EXP_WIN), ((0, 32),), -0.2, 0.2), 0.2, 1.0)
    gate_up_weight = normal_values(key_of[4], (N_EXPERT, D, 2 * F_DEV), D ** -0.5, 0.09375, ((0, 8), (1, 4)))
    down_weight = normal_values(key_of[5], (N_EXPERT, F_DEV, D), F ** -0.5, 0.15625, ((0, 8), (2, 4)))
    return {"tokens": tokens, "output_gradient": output_gradient, "slot": slot, "gate_weight": gate_weight, "gate_up_weight": gate_up_weight, "down_weight": down_weight}


def expert_slice(x_mat, g_mat, gate_up, down):
    joined = jnp.dot(x_mat, gate_up, preferred_element_type=jnp.float32)
    half = gate_up.shape[1] // 2
    pre = joined[:, :half]
    up = joined[:, half:]
    sig = jax.nn.sigmoid(pre)
    act = pre * sig
    dh = lax.dot_general(g_mat, down, (((1,), (1,)), ((), ())), preferred_element_type=jnp.float32)
    dgate = dh * up * sig * (1.0 + pre * (1.0 - sig))
    dup = dh * act
    dgu = jnp.concatenate([dgate, dup], axis=1).astype(jnp.bfloat16)
    dx_part = lax.dot_general(dgu, gate_up, (((1,), (1,)), ((), ())), preferred_element_type=jnp.float32).astype(jnp.bfloat16)
    part_gu = lax.dot_general(x_mat, dgu, (((0,), (0,)), ((), ())), preferred_element_type=jnp.float32).astype(jnp.bfloat16)
    return dx_part, part_gu


def reference(tokens, output_gradient, slot, gate_weight, gate_up_weight, down_weight):
    x_all = tokens.reshape(N_DP, N_EXPERT, TOK_DEV, D)
    g_all = output_gradient.reshape(N_DP, N_EXPERT, TOK_DEV, D)
    s_all = slot.reshape(N_DP, N_EXPERT, TOK_DEV, EXP_WIN)
    w_all = gate_weight.reshape(N_DP, N_EXPERT, TOK_DEV, EXP_WIN)
    positions = jnp.arange(CAP, dtype=jnp.int32)

    def per_replica(acc_gu, inputs):
        x_d, g_d, s_d, down_matrix = inputs
        selector = jnp.transpose(s_d, (0, 2, 1))[:, :, None, :] == positions[None, None, :, None]
        picked_experts = selector.astype(jnp.float32)
        rows_x = jnp.einsum('iect,itd->iecd', picked_experts, x_d.astype(jnp.float32)).astype(jnp.bfloat16)
        rows_dy = jnp.einsum('iect,itd->iecd', picked_experts, g_d.astype(jnp.float32))
        selected_gate = jnp.einsum('ovjb,obv->ovj', picked_experts, down_matrix)
        rows_g = (rows_dy * selected_gate[..., None]).astype(jnp.bfloat16)
        grad_x = jnp.zeros((N_EXPERT, TOK_DEV, D), jnp.float32)
        parts_gu = []
        for expert in range(EXP_WIN):
            x_mat = rows_x[:, expert].reshape(N_EXPERT * CAP, D)
            g_mat = rows_g[:, expert].reshape(N_EXPERT * CAP, D)
            total = jnp.zeros((N_EXPERT * CAP, D), jnp.float32)
            for piece in range(GROUP):
                index = expert * GROUP + piece
                dx_part, part_gu = expert_slice(x_mat, g_mat, gate_up_weight[index], down_weight[index])
                total = total + lax.optimization_barrier(dx_part).astype(jnp.float32)
                parts_gu.append(lax.optimization_barrier(part_gu).astype(jnp.float32))
            grad_x = grad_x + jnp.einsum('ict,icd->itd', picked_experts[:, expert], total.reshape(N_EXPERT, CAP, D))
        acc_gu = acc_gu + jnp.stack(parts_gu)
        return acc_gu, grad_x.astype(jnp.bfloat16)

    start = jnp.zeros((N_EXPERT, D, 2 * F_DEV), jnp.float32)
    acc_gu, grad_x = lax.scan(per_replica, start, (x_all, g_all, s_all, w_all))
    grad_tokens = grad_x.reshape(TOKENS, D)
    return grad_tokens, acc_gu.astype(jnp.bfloat16)
```

```python
import functools

import jax
import jax.numpy as jnp
from jax import lax
from jax.experimental import pallas as pl
from jax.experimental.pallas import tpu as pltpu
from jax.sharding import PartitionSpec as P

GROUP = 8
CAP = 8
MESH = pl.DeviceIdType.MESH
F32 = jnp.float32
BF16 = jnp.bfloat16
NT = (((1,), (1,)), ((), ()))
TN = (((0,), (0,)), ((), ()))


def kernel(
    n_dp, windows,
    tok_ref, dy_ref, slot_ref, gate_ref, gu_ref, down_ref,
    gx_ref, gw_ref,
    pick, buf, xall, part, prcv, dgrcv, dguall, dxs, ret, back, fin,
    s_pick, r_pick, s_ag, r_ag, s_rs, r_rs, s_dg, r_dg, s_ret, r_ret, s_fin, r_fin,
):
    S = GROUP
    Z = S // 2
    W = windows
    n_same = n_dp * W
    tokens, width = tok_ref.shape
    cols = width // n_dp
    hidden = down_ref.shape[0]
    rows = n_dp * W * CAP
    me_d = lax.axis_index("dp")
    me_x = lax.axis_index("expert")
    me_w = me_x // S
    me_s = me_x % S
    zz = me_s // 2
    yy = me_s % 2

    def member(s):
        return (me_d, me_w * S + s)

    barrier = pltpu.get_barrier_semaphore()

    def same(k):
        flat = (me_d * W + me_w + k) % n_same
        return flat // W, flat % W

    for k in range(1, n_same):
        d, w = same(k)
        pl.semaphore_signal(barrier, inc=1, device_id=(d, w * S + me_s), device_id_type=MESH)
    for k in range(1, S):
        pl.semaphore_signal(barrier, inc=1, device_id=member((me_s + k) % S), device_id_type=MESH)

    lane = lax.broadcasted_iota(jnp.int32, (tokens, 128), 1)
    for e in range(W):
        hit = slot_ref[:, e : e + 1] == lane
        sel = jnp.where(hit, 1.0, 0.0).T[:CAP]
        weight = jnp.sum(jnp.where(hit, gate_ref[:, e : e + 1], 0.0).T[:CAP], axis=1, keepdims=True)
        sel = sel.astype(BF16)
        for d in range(n_dp):
            cut = slice(d * cols, (d + 1) * cols)
            x = jnp.dot(sel, tok_ref[:, cut], preferred_element_type=F32)
            g = jnp.dot(sel, dy_ref[:, cut], preferred_element_type=F32) * weight
            pick[d, e] = jnp.concatenate([x, g], axis=0).astype(BF16)
    pl.semaphore_wait(barrier, n_same - 1 + S - 1)

    def pick_copy(d, w):
        return pltpu.make_async_remote_copy(
            src_ref=pick.at[d, w], dst_ref=buf.at[me_s, me_d, me_w],
            send_sem=s_pick.at[d, w], recv_sem=r_pick.at[me_d, me_w],
            device_id=(d, w * S + me_s), device_id_type=MESH,
        )

    def pick_arrival(d, w):
        return pltpu.make_async_remote_copy(
            src_ref=pick.at[d, w], dst_ref=buf.at[me_s, d, w],
            send_sem=s_pick.at[d, w], recv_sem=r_pick.at[d, w],
            device_id=(d, w * S + me_s), device_id_type=MESH,
        )

    for k in range(1, n_same):
        pick_copy(*same(k)).start()
    buf[me_s, me_d, me_w] = pick[me_d, me_w]
    for k in range(1, n_same):
        pick_arrival(*same(k)).wait_recv()

    def spread(slot, way, target):
        return pltpu.make_async_remote_copy(
            src_ref=buf.at[slot], dst_ref=buf.at[slot],
            send_sem=s_ag.at[slot, way], recv_sem=r_ag.at[slot],
            device_id=member(target), device_id_type=MESH,
        )

    def reduce_copy(slot, d, owner):
        return pltpu.make_async_remote_copy(
            src_ref=part.at[slot, d], dst_ref=prcv.at[slot, owner],
            send_sem=s_rs.at[slot, d], recv_sem=r_rs.at[slot, owner],
            device_id=(d, me_x), device_id_type=MESH,
        )

    def share_copy(slot, d, owner):
        return pltpu.make_async_remote_copy(
            src_ref=dgrcv.at[slot, me_d], dst_ref=dgrcv.at[slot, owner],
            send_sem=s_dg.at[slot, d], recv_sem=r_dg.at[slot, owner],
            device_id=(d, me_x), device_id_type=MESH,
        )

    def return_copy(slot, owner):
        return pltpu.make_async_remote_copy(
            src_ref=dxs.at[slot], dst_ref=ret.at[owner],
            send_sem=s_ret.at[slot], recv_sem=r_ret.at[owner],
            device_id=member(slot), device_id_type=MESH,
        )

    near = jnp.minimum(zz, Z - 1 - zz)

    def nth(n):
        m = n // 2
        alternating = ((m + 1) // 2) * (1 - 2 * (m % 2))
        far = m - near
        beyond = jnp.where(zz > Z - 1 - zz, -far, far)
        delta = jnp.where(m <= 2 * near, alternating, beyond)
        own = n % 2 == 0
        return delta, own, (zz + delta) * 2 + jnp.where(own, yy, 1 - yy)

    def up(delta, own):
        return own & (delta <= 0) & (zz + 1 < Z)

    def down(delta, own):
        return own & (delta >= 0) & (zz >= 1)

    def arrive(n):
        delta, own, slot = nth(n)

        @pl.when(n > 0)
        def _():
            spread(slot, 0, (me_s + 1) % S).wait_recv()

        @pl.when(up(delta, own))
        def _():
            spread(slot, 0, me_s + 2).start()

        @pl.when(down(delta, own))
        def _():
            spread(slot, 1, me_s - 2).start()

        @pl.when(own)
        def _():
            spread(slot, 2, zz * 2 + 1 - yy).start()

        both = buf[slot].astype(F32).reshape(n_dp * W, 2, CAP, cols)
        x = both[:, 0].reshape(rows, cols).astype(BF16)
        g = both[:, 1].reshape(rows, cols).astype(BF16)
        xall[slot] = x
        a_u = jnp.dot(x, gu_ref[...], preferred_element_type=F32)
        dh = lax.dot_general(g, down_ref[...], NT, preferred_element_type=F32)
        part[slot, :, :, : 2 * hidden] = a_u.reshape(n_dp, W * CAP, 2 * hidden)
        part[slot, :, :, 2 * hidden :] = dh.reshape(n_dp, W * CAP, hidden)
        for k in range(1, n_dp):
            reduce_copy(slot, (me_d + k) % n_dp, me_d).start()

    def activate(n):
        _, _, slot = nth(n)
        total = part[slot, me_d]
        for k in range(1, n_dp):
            d = (me_d + k) % n_dp
            reduce_copy(slot, d, d).wait_recv()
            total = total + prcv[slot, d]
        pre = total[:, :hidden]
        up_part = total[:, hidden : 2 * hidden]
        dh = total[:, 2 * hidden :]
        sig = jax.nn.sigmoid(pre)
        dgate = dh * up_part * sig * (1.0 + pre * (1.0 - sig))
        dup = dh * (pre * sig)
        dgrcv[slot, me_d] = jnp.concatenate(
            [dgate.reshape(W, CAP, hidden), dup.reshape(W, CAP, hidden)], axis=1
        ).astype(BF16)
        for k in range(1, n_dp):
            share_copy(slot, (me_d + k) % n_dp, me_d).start()

    def give_back(n):
        _, _, slot = nth(n)
        for k in range(1, n_dp):
            d = (me_d + k) % n_dp
            share_copy(slot, d, d).wait_recv()
        both = dgrcv[slot].astype(F32).reshape(n_dp * W, 2, CAP, hidden)
        dgu = jnp.concatenate(
            [both[:, 0].reshape(rows, hidden), both[:, 1].reshape(rows, hidden)], axis=1
        ).astype(BF16)
        dguall[slot] = dgu
        dxs[slot] = lax.dot_general(dgu, gu_ref[...], NT, preferred_element_type=F32).astype(BF16)

        @pl.when(n > 0)
        def _():
            return_copy(slot, me_s).start()

    def step(n, carry):
        @pl.when(n < S)
        def _():
            arrive(n)

        @pl.when((n >= 1) & (n < S + 1))
        def _():
            activate(n - 1)

        @pl.when(n >= 2)
        def _():
            give_back(n - 2)

        return carry

    lax.fori_loop(0, S + 2, step, 0)

    gw_ref[0] = lax.dot_general(
        xall[...].reshape(S * rows, cols), dguall[...].reshape(S * rows, 2 * hidden), TN,
        preferred_element_type=F32,
    ).astype(BF16)

    total = dxs[me_s].astype(F32)
    for k in range(1, S):
        s = (me_s + k) % S
        return_copy(s, s).wait_recv()
        total = total + ret[s].astype(F32)
    total = total.reshape(n_dp, W, CAP, cols)
    back[...] = jnp.concatenate(
        [total[..., : cols // 2], total[..., cols // 2 :]], axis=2
    ).astype(BF16)

    def fin_copy(d, w, owner_d, owner_w):
        return pltpu.make_async_remote_copy(
            src_ref=back.at[d, w], dst_ref=fin.at[owner_d, owner_w],
            send_sem=s_fin.at[d, w], recv_sem=r_fin.at[owner_d, owner_w],
            device_id=(d, w * S + me_s), device_id_type=MESH,
        )

    for k in range(1, n_same):
        d, w = same(k)
        fin_copy(d, w, me_d, me_w).start()
    fin[me_d, me_w] = back[me_d, me_w]
    for k in range(1, n_same):
        d, w = same(k)
        fin_copy(d, w, d, w).wait_recv()

    lane16 = lax.broadcasted_iota(jnp.int32, (tokens, 2 * CAP), 1)
    for d in range(n_dp):
        for h in range(2):
            out = jnp.zeros((tokens, cols // 2), F32)
            for e in range(W):
                hit = slot_ref[:, e : e + 1] == lane16 - h * CAP
                pos = jnp.where(hit & (lane16 >= h * CAP), 1.0, 0.0).astype(BF16)
                out = out + jnp.dot(pos, fin[d, e], preferred_element_type=F32)
            at = d * cols + h * (cols // 2)
            gx_ref[:, at : at + cols // 2] = out.astype(BF16)

    for k in range(1, n_same):
        d, w = same(k)
        pick_copy(d, w).wait_send()
        fin_copy(d, w, me_d, me_w).wait_send()
    for k in range(1, S):
        return_copy((me_s + k) % S, me_s).wait_send()

    def drain(n, carry):
        delta, own, slot = nth(n)

        @pl.when(up(delta, own))
        def _():
            spread(slot, 0, me_s + 2).wait_send()

        @pl.when(down(delta, own))
        def _():
            spread(slot, 1, me_s - 2).wait_send()

        @pl.when(own)
        def _():
            spread(slot, 2, zz * 2 + 1 - yy).wait_send()

        for k in range(1, n_dp):
            d = (me_d + k) % n_dp
            reduce_copy(slot, d, me_d).wait_send()
            share_copy(slot, d, me_d).wait_send()
        return carry

    lax.fori_loop(0, S, drain, 0)


def on_device(n_dp, tokens, output_gradient, slot, gate_weight, gate_up_weight, down_weight):
    W = slot.shape[1]
    S = GROUP
    width = tokens.shape[1]
    _, cols, wide = gate_up_weight.shape
    hidden = wide // 2
    rows = n_dp * W * CAP
    vmem = pl.BlockSpec(memory_space=pltpu.VMEM)
    dma = pltpu.SemaphoreType.DMA
    flops = 2 * S * rows * cols * hidden * 7
    return pl.pallas_call(
        functools.partial(kernel, n_dp, W),
        out_shape=(
            jax.ShapeDtypeStruct(tokens.shape, BF16),
            jax.ShapeDtypeStruct(gate_up_weight.shape, BF16),
        ),
        in_specs=[vmem] * 6,
        out_specs=(vmem, vmem),
        scratch_shapes=[
            pltpu.VMEM((n_dp, W, 2 * CAP, cols), BF16),
            pltpu.VMEM((S, n_dp, W, 2 * CAP, cols), BF16),
            pltpu.VMEM((S, rows, cols), BF16),
            pltpu.VMEM((S, n_dp, W * CAP, 3 * hidden), F32),
            pltpu.VMEM((S, n_dp, W * CAP, 3 * hidden), F32),
            pltpu.VMEM((S, n_dp, W, 2 * CAP, hidden), BF16),
            pltpu.VMEM((S, rows, wide), BF16),
            pltpu.VMEM((S, rows, cols), BF16),
            pltpu.VMEM((S, rows, cols), BF16),
            pltpu.VMEM((n_dp, W, 2 * CAP, cols // 2), BF16),
            pltpu.VMEM((n_dp, W, 2 * CAP, cols // 2), BF16),
            dma((n_dp, W)), dma((n_dp, W)),
            dma((S, 3)), dma((S,)),
            dma((S, n_dp)), dma((S, n_dp)),
            dma((S, n_dp)), dma((S, n_dp)),
            dma((S,)), dma((S,)),
            dma((n_dp, W)), dma((n_dp, W)),
        ],
        compiler_params=pltpu.CompilerParams(
            collective_id=0, has_side_effects=True, vmem_limit_bytes=58 * 1024 * 1024
        ),
        cost_estimate=pl.CostEstimate(
            flops=flops, bytes_accessed=6 * tokens.size + 4 * gate_up_weight.size, transcendentals=0
        ),
        name="routed_backward",
    )(tokens, output_gradient, slot, gate_weight, gate_up_weight[0], down_weight[0])


def solution(mesh):
    in_specs = (
        P(("dp", "expert"), None),
        P(("dp", "expert"), None),
        P(("dp", "expert"), None),
        P(("dp", "expert"), None),
        P("expert", "dp", None),
        P("expert", None, "dp"),
    )
    out_specs = (P(("dp", "expert"), None), P("expert", "dp", None))
    return jax.shard_map(
        functools.partial(on_device, mesh.shape["dp"]),
        mesh=mesh, in_specs=in_specs, out_specs=out_specs, check_vma=False,
    )
```

```python
import functools

import jax
import jax.numpy as jnp
from jax import lax
from jax.experimental import pallas as pl
from jax.experimental.pallas import tpu as pltpu
from jax.sharding import PartitionSpec as P

GROUP = 8
CAP = 8
MESH = pl.DeviceIdType.MESH
F32 = jnp.float32
BF16 = jnp.bfloat16
NT = (((1,), (1,)), ((), ()))
TN = (((0,), (0,)), ((), ()))


def kernel(
    n_dp, windows,
    tok_ref, dy_ref, slot_ref, gate_ref, gu_ref, down_ref,
    fin_ref, gw_ref,
    pick, buf, xall, part, prcv, dgrcv, dguall, dxs, ret, back, fin, gut, downt,
    s_pick, r_pick, s_ag, r_ag, s_rs, r_rs, s_dg, r_dg, s_ret, r_ret, s_fin, r_fin,
):
    S = GROUP
    Z = S // 2
    W = windows
    n_same = n_dp * W
    tokens, width = tok_ref.shape
    cols = width // n_dp
    hidden = down_ref.shape[0]
    rows = n_dp * W * CAP
    me_d = lax.axis_index("dp")
    me_x = lax.axis_index("expert")
    me_w = me_x // S
    me_s = me_x % S
    zz = me_s // 2
    yy = me_s % 2

    def member(z, y):
        return (me_d, me_w * S + z * 2 + y)

    barrier = pltpu.get_barrier_semaphore()

    def same(k):
        flat = (me_d * W + me_w + k) % n_same
        return flat // W, flat % W

    def other(k):
        s = (me_s + k) % S
        return s // 2, s % 2

    for k in range(1, n_same):
        d, w = same(k)
        pl.semaphore_signal(barrier, inc=1, device_id=(d, w * S + me_s), device_id_type=MESH)
    for k in range(1, S):
        pl.semaphore_signal(barrier, inc=1, device_id=member(*other(k)), device_id_type=MESH)

    place = lax.broadcasted_iota(jnp.int32, (CAP, tokens), 0)
    for e in range(W):
        hit = slot_ref[e : e + 1, :] == place
        sel = jnp.where(hit, 1.0, 0.0).astype(BF16)
        weight = jnp.sum(jnp.where(hit, gate_ref[e : e + 1, :], 0.0), axis=1, keepdims=True)
        for d in range(n_dp):
            cut = slice(d * cols, (d + 1) * cols)
            x = jnp.dot(sel, tok_ref[:, cut], preferred_element_type=F32)
            g = jnp.dot(sel, dy_ref[:, cut], preferred_element_type=F32) * weight
            pick[d, e] = jnp.concatenate([x, g], axis=0).astype(BF16)
    pl.semaphore_wait(barrier, n_same - 1 + S - 1)

    def pick_copy(d, w):
        return pltpu.make_async_remote_copy(
            src_ref=pick.at[d, w], dst_ref=buf.at[zz, yy, me_d, me_w],
            send_sem=s_pick.at[d, w], recv_sem=r_pick.at[me_d, me_w],
            device_id=(d, w * S + me_s), device_id_type=MESH,
        )

    def pick_arrival(d, w):
        return pltpu.make_async_remote_copy(
            src_ref=pick.at[d, w], dst_ref=buf.at[zz, yy, d, w],
            send_sem=s_pick.at[d, w], recv_sem=r_pick.at[d, w],
            device_id=(d, w * S + me_s), device_id_type=MESH,
        )

    for k in range(1, n_same):
        pick_copy(*same(k)).start()
    buf[zz, yy, me_d, me_w] = pick[me_d, me_w]
    downt[...] = down_ref[...].T
    for k in range(1, n_same):
        pick_arrival(*same(k)).wait_recv()

    def spread(z, y, way, target):
        return pltpu.make_async_remote_copy(
            src_ref=buf.at[z, y], dst_ref=buf.at[z, y],
            send_sem=s_ag.at[z, way], recv_sem=r_ag.at[z, y],
            device_id=member(*target), device_id_type=MESH,
        )

    def reduce_copy(z, d, owner):
        return pltpu.make_async_remote_copy(
            src_ref=part.at[z, d], dst_ref=prcv.at[z, owner],
            send_sem=s_rs.at[z, d], recv_sem=r_rs.at[z, owner],
            device_id=(d, me_x), device_id_type=MESH,
        )

    def share_copy(z, d, owner):
        return pltpu.make_async_remote_copy(
            src_ref=dgrcv.at[z, me_d], dst_ref=dgrcv.at[z, owner],
            send_sem=s_dg.at[z, d], recv_sem=r_dg.at[z, owner],
            device_id=(d, me_x), device_id_type=MESH,
        )

    def return_copy(z, y, owner_z, owner_y):
        return pltpu.make_async_remote_copy(
            src_ref=dxs.at[z, y], dst_ref=ret.at[owner_z, owner_y],
            send_sem=s_ret.at[z, y], recv_sem=r_ret.at[owner_z, owner_y],
            device_id=member(z, y), device_id_type=MESH,
        )

    near = jnp.minimum(zz, Z - 1 - zz)

    def nth(m):
        alternating = ((m + 1) // 2) * (1 - 2 * (m % 2))
        far = m - near
        beyond = jnp.where(zz > Z - 1 - zz, -far, far)
        return zz + jnp.where(m <= 2 * near, alternating, beyond)

    def forward(z, act):
        @pl.when((z <= zz) & (zz + 1 < Z))
        def _():
            act(spread(z, yy, 0, (zz + 1, yy)))

        @pl.when((z >= zz) & (zz >= 1))
        def _():
            act(spread(z, yy, 1, (zz - 1, yy)))

        act(spread(z, yy, 2, (zz, 1 - yy)))

    def start(copy):
        copy.start()

    def pass_on(k):
        @pl.when(zz - k >= 0)
        def _():
            spread(zz - k, yy, 2, (zz, 1 - yy)).wait_recv()
            forward(zz - k, start)

        @pl.when(zz + k < Z)
        def _():
            spread(zz + k, yy, 2, (zz, 1 - yy)).wait_recv()
            forward(zz + k, start)

    def arrive(m):
        z = nth(m)
        spread(z, 1 - yy, 2, (zz, 1 - yy)).wait_recv()
        both = buf[z].astype(F32).reshape(2 * n_dp * W, 2, CAP, cols)
        x = both[:, 0].reshape(2 * rows, cols).astype(BF16)
        g = both[:, 1].reshape(2 * rows, cols).astype(BF16)
        xall[z] = x
        a_u = jnp.dot(x, gu_ref[...], preferred_element_type=F32)
        a_u = a_u.reshape(2, n_dp, W * CAP, 2 * hidden)
        dh = jnp.dot(g, downt[...], preferred_element_type=F32)
        dh = dh.reshape(2, n_dp, W * CAP, hidden)
        part[z, :, :, : 2 * hidden] = jnp.concatenate([a_u[0], a_u[1]], axis=1).astype(BF16)
        part[z, :, :, 2 * hidden :] = jnp.concatenate([dh[0], dh[1]], axis=1).astype(BF16)
        for k in range(1, n_dp):
            reduce_copy(z, (me_d + k) % n_dp, me_d).start()

    def activate(m):
        z = nth(m)
        total = part[z, me_d].astype(F32)
        for k in range(1, n_dp):
            d = (me_d + k) % n_dp
            reduce_copy(z, d, d).wait_recv()
            total = total + prcv[z, d].astype(F32)
        pre = total[:, :hidden]
        up_part = total[:, hidden : 2 * hidden]
        dh = total[:, 2 * hidden :]
        sig = jax.nn.sigmoid(pre)
        dgate = dh * up_part * sig * (1.0 + pre * (1.0 - sig))
        dup = dh * (pre * sig)
        dgrcv[z, me_d] = jnp.concatenate(
            [dgate.reshape(2 * W, CAP, hidden), dup.reshape(2 * W, CAP, hidden)], axis=1
        ).astype(BF16)
        for k in range(1, n_dp):
            share_copy(z, (me_d + k) % n_dp, me_d).start()

    def give_back(m):
        z = nth(m)
        for k in range(1, n_dp):
            d = (me_d + k) % n_dp
            share_copy(z, d, d).wait_recv()
        both = dgrcv[z].astype(F32).reshape(n_dp, 2, W, 2, CAP, hidden)
        dgate = jnp.concatenate([both[:, y, :, 0].reshape(rows, hidden) for y in range(2)], axis=0)
        dup = jnp.concatenate([both[:, y, :, 1].reshape(rows, hidden) for y in range(2)], axis=0)
        dgu = jnp.concatenate([dgate, dup], axis=1).astype(BF16)
        dguall[z] = dgu
        dx = jnp.dot(dgu, gut[...], preferred_element_type=F32).astype(BF16)
        dxs[z] = dx.reshape(2, rows, cols)
        return_copy(z, 1 - yy, zz, yy).start()

        @pl.when(m > 0)
        def _():
            return_copy(z, yy, zz, yy).start()

    def step(m, carry):
        @pl.when(m < Z)
        def _():
            pass_on(m + 1)
            arrive(m)

        @pl.when((m >= 1) & (m < Z + 1))
        def _():
            activate(m - 1)

        @pl.when(m >= 2)
        def _():
            give_back(m - 2)

        return carry

    forward(zz, start)
    gut[...] = gu_ref[...].T
    lax.fori_loop(0, Z + 2, step, 0)

    gw_ref[0] = lax.dot_general(
        xall[...].reshape(S * rows, cols), dguall[...].reshape(S * rows, 2 * hidden), TN,
        preferred_element_type=F32,
    ).astype(BF16)

    total = dxs[zz, yy].astype(F32)
    for k in range(1, S):
        z, y = other(k)
        return_copy(z, y, z, y).wait_recv()
        total = total + ret[z, y].astype(F32)
    total = total.reshape(n_dp, W, CAP, cols)
    back[...] = jnp.concatenate(
        [total[..., : cols // 2], total[..., cols // 2 :]], axis=2
    ).astype(BF16)

    def fin_copy(d, w, owner_d, owner_w):
        return pltpu.make_async_remote_copy(
            src_ref=back.at[d, w], dst_ref=fin.at[owner_d, owner_w],
            send_sem=s_fin.at[d, w], recv_sem=r_fin.at[owner_d, owner_w],
            device_id=(d, w * S + me_s), device_id_type=MESH,
        )

    for k in range(1, n_same):
        d, w = same(k)
        fin_copy(d, w, me_d, me_w).start()
    fin[me_d, me_w] = back[me_d, me_w]

    for k in range(1, n_same):
        pick_copy(*same(k)).wait_send()
    for k in range(1, S):
        z, y = other(k)
        return_copy(z, y, zz, yy).wait_send()

    def wait_send(copy):
        copy.wait_send()

    def drain(z, carry):
        forward(z, wait_send)
        for k in range(1, n_dp):
            d = (me_d + k) % n_dp
            reduce_copy(z, d, me_d).wait_send()
            share_copy(z, d, me_d).wait_send()
        return carry

    lax.fori_loop(0, Z, drain, 0)
    for k in range(1, n_same):
        d, w = same(k)
        fin_copy(d, w, d, w).wait_recv()
        fin_copy(d, w, me_d, me_w).wait_send()
    fin_ref[...] = fin[...]


def place_rows(fin_ref, slot_ref, gx_ref):
    n_dp, W, _, half = fin_ref.shape
    tokens = gx_ref.shape[0]
    place = lax.broadcasted_iota(jnp.int32, (2 * CAP, tokens), 0)
    for h in range(2):
        hits = []
        for e in range(W):
            hit = (slot_ref[e : e + 1, :] == place - h * CAP) & (place >= h * CAP)
            hits.append(jnp.where(hit, 1.0, 0.0).T.astype(BF16))
        for d in range(n_dp):
            out = jnp.dot(hits[0], fin_ref[d, 0], preferred_element_type=F32)
            for e in range(1, W):
                out = out + jnp.dot(hits[e], fin_ref[d, e], preferred_element_type=F32)
            at = (2 * d + h) * half
            gx_ref[:, at : at + half] = out.astype(BF16)


def on_device(n_dp, tokens, output_gradient, slot, gate_weight, gate_up_weight, down_weight):
    W = slot.shape[1]
    S = GROUP
    Z = S // 2
    _, cols, wide = gate_up_weight.shape
    hidden = wide // 2
    rows = n_dp * W * CAP
    vmem = pl.BlockSpec(memory_space=pltpu.VMEM)
    dma = pltpu.SemaphoreType.DMA
    slot_row = slot.T
    fin, grad_gate_up = pl.pallas_call(
        functools.partial(kernel, n_dp, W),
        out_shape=(
            jax.ShapeDtypeStruct((n_dp, W, 2 * CAP, cols // 2), BF16),
            jax.ShapeDtypeStruct(gate_up_weight.shape, BF16),
        ),
        in_specs=[vmem] * 6,
        out_specs=(vmem, vmem),
        scratch_shapes=[
            pltpu.VMEM((n_dp, W, 2 * CAP, cols), BF16),
            pltpu.VMEM((Z, 2, n_dp, W, 2 * CAP, cols), BF16),
            pltpu.VMEM((Z, 2 * rows, cols), BF16),
            pltpu.VMEM((Z, n_dp, 2 * W * CAP, 3 * hidden), BF16),
            pltpu.VMEM((Z, n_dp, 2 * W * CAP, 3 * hidden), BF16),
            pltpu.VMEM((Z, n_dp, 2 * W, 2 * CAP, hidden), BF16),
            pltpu.VMEM((Z, 2 * rows, wide), BF16),
            pltpu.VMEM((Z, 2, rows, cols), BF16),
            pltpu.VMEM((Z, 2, rows, cols), BF16),
            pltpu.VMEM((n_dp, W, 2 * CAP, cols // 2), BF16),
            pltpu.VMEM((n_dp, W, 2 * CAP, cols // 2), BF16),
            pltpu.VMEM((wide, cols), BF16),
            pltpu.VMEM((cols, hidden), BF16),
            dma((n_dp, W)), dma((n_dp, W)),
            dma((Z, 3)), dma((Z, 2)),
            dma((Z, n_dp)), dma((Z, n_dp)),
            dma((Z, n_dp)), dma((Z, n_dp)),
            dma((Z, 2)), dma((Z, 2)),
            dma((n_dp, W)), dma((n_dp, W)),
        ],
        compiler_params=pltpu.CompilerParams(
            collective_id=0, has_side_effects=True, vmem_limit_bytes=58 * 1024 * 1024
        ),
        cost_estimate=pl.CostEstimate(
            flops=14 * S * rows * cols * hidden,
            bytes_accessed=4 * tokens.size + 4 * gate_up_weight.size, transcendentals=0,
        ),
        name="routed_backward",
    )(tokens, output_gradient, slot_row, gate_weight.T, gate_up_weight[0], down_weight[0])
    grad_tokens = pl.pallas_call(
        place_rows,
        out_shape=jax.ShapeDtypeStruct(tokens.shape, BF16),
        in_specs=[vmem] * 2,
        out_specs=vmem,
        compiler_params=pltpu.CompilerParams(vmem_limit_bytes=32 * 1024 * 1024),
        name="place_rows",
    )(fin, slot_row)
    return grad_tokens, grad_gate_up


def solution(mesh):
    in_specs = (
        P(("dp", "expert"), None),
        P(("dp", "expert"), None),
        P(("dp", "expert"), None),
        P(("dp", "expert"), None),
        P("expert", "dp", None),
        P("expert", None, "dp"),
    )
    out_specs = (P(("dp", "expert"), None), P("expert", "dp", None))
    return jax.shard_map(
        functools.partial(on_device, mesh.shape["dp"]),
        mesh=mesh, in_specs=in_specs, out_specs=out_specs, check_vma=False,
    )
```

```python
import functools

import jax
import jax.numpy as jnp
from jax import lax
from jax.experimental import pallas as pl
from jax.experimental.pallas import tpu as pltpu
from jax.sharding import PartitionSpec as P

GROUP = 8
CAP = 8
MESH = pl.DeviceIdType.MESH
F32 = jnp.float32
BF16 = jnp.bfloat16
NT = (((1,), (1,)), ((), ()))
TN = (((0,), (0,)), ((), ()))


def kernel(
    n_dp, windows,
    tok_ref, dy_ref, slot_ref, gate_ref, gu_ref, down_ref,
    fin_ref, gw_ref,
    pick, buf, xall, part, prcv, dgrcv, dguall, dxs, ret, back, fin, gut, downt,
    s_pick, r_pick, s_ag, r_ag, s_rs, r_rs, s_dg, r_dg, s_ret, r_ret, s_fin, r_fin,
):
    S = GROUP
    Z = S // 2
    W = windows
    n_same = n_dp * W
    tokens, width = tok_ref.shape
    cols = width // n_dp
    half = cols // 2
    hidden = down_ref.shape[0]
    rows = n_dp * W * CAP
    me_d = lax.axis_index("dp")
    me_x = lax.axis_index("expert")
    me_w = me_x // S
    me_s = me_x % S
    zz = me_s // 2
    yy = me_s % 2

    def member(z, y):
        return (me_d, me_w * S + z * 2 + y)

    barrier = pltpu.get_barrier_semaphore()

    def same(k):
        flat = (me_d * W + me_w + k) % n_same
        return flat // W, flat % W

    def other(k):
        s = (me_s + k) % S
        return s // 2, s % 2

    for k in range(1, n_same):
        d, w = same(k)
        pl.semaphore_signal(barrier, inc=1, device_id=(d, w * S + me_s), device_id_type=MESH)
    for k in range(1, S):
        pl.semaphore_signal(barrier, inc=1, device_id=member(*other(k)), device_id_type=MESH)

    def pick_copy(h, d, w):
        return pltpu.make_async_remote_copy(
            src_ref=pick.at[h, d, w], dst_ref=buf.at[zz, yy, h, me_d, me_w],
            send_sem=s_pick.at[h, d, w], recv_sem=r_pick.at[h, me_d, me_w],
            device_id=(d, w * S + me_s), device_id_type=MESH,
        )

    def pick_arrival(h, d, w):
        return pltpu.make_async_remote_copy(
            src_ref=pick.at[h, d, w], dst_ref=buf.at[zz, yy, h, d, w],
            send_sem=s_pick.at[h, d, w], recv_sem=r_pick.at[h, d, w],
            device_id=(d, w * S + me_s), device_id_type=MESH,
        )

    place = lax.broadcasted_iota(jnp.int32, (CAP, tokens), 0)
    sels, weights = [], []
    for e in range(W):
        hit = slot_ref[e : e + 1, :] == place
        sels.append(jnp.where(hit, 1.0, 0.0).astype(BF16))
        weights.append(
            jnp.sum(jnp.where(hit, gate_ref[e : e + 1, :], 0.0), axis=1, keepdims=True)
        )
    for h in range(2):
        for e in range(W):
            for d in range(n_dp):
                cut = slice(d * cols + h * half, d * cols + (h + 1) * half)
                x = jnp.dot(sels[e], tok_ref[:, cut], preferred_element_type=F32)
                g = jnp.dot(sels[e], dy_ref[:, cut], preferred_element_type=F32) * weights[e]
                pick[h, d, e] = jnp.concatenate([x, g], axis=0).astype(BF16)
        if h == 0:
            pl.semaphore_wait(barrier, n_same - 1 + S - 1)
        for k in range(1, n_same):
            pick_copy(h, *same(k)).start()
        buf[zz, yy, h, me_d, me_w] = pick[h, me_d, me_w]
    downt[...] = down_ref[...].T

    def spread(z, y, h, way, target):
        return pltpu.make_async_remote_copy(
            src_ref=buf.at[z, y, h], dst_ref=buf.at[z, y, h],
            send_sem=s_ag.at[z, h, way], recv_sem=r_ag.at[z, y, h],
            device_id=member(*target), device_id_type=MESH,
        )

    def reduce_copy(z, d, owner):
        return pltpu.make_async_remote_copy(
            src_ref=part.at[z, d], dst_ref=prcv.at[z, owner],
            send_sem=s_rs.at[z, d], recv_sem=r_rs.at[z, owner],
            device_id=(d, me_x), device_id_type=MESH,
        )

    def share_copy(z, d, owner):
        return pltpu.make_async_remote_copy(
            src_ref=dgrcv.at[z, me_d], dst_ref=dgrcv.at[z, owner],
            send_sem=s_dg.at[z, d], recv_sem=r_dg.at[z, owner],
            device_id=(d, me_x), device_id_type=MESH,
        )

    def return_copy(z, y, owner_z, owner_y):
        return pltpu.make_async_remote_copy(
            src_ref=dxs.at[z, y], dst_ref=ret.at[owner_z, owner_y],
            send_sem=s_ret.at[z, y], recv_sem=r_ret.at[owner_z, owner_y],
            device_id=member(z, y), device_id_type=MESH,
        )

    near = jnp.minimum(zz, Z - 1 - zz)

    def nth(m):
        alternating = ((m + 1) // 2) * (1 - 2 * (m % 2))
        far = m - near
        beyond = jnp.where(zz > Z - 1 - zz, -far, far)
        return zz + jnp.where(m <= 2 * near, alternating, beyond)

    def forward(z, h, act):
        @pl.when((z <= zz) & (zz + 1 < Z))
        def _():
            act(spread(z, yy, h, 0, (zz + 1, yy)))

        @pl.when((z >= zz) & (zz >= 1))
        def _():
            act(spread(z, yy, h, 1, (zz - 1, yy)))

        act(spread(z, yy, h, 2, (zz, 1 - yy)))

    def start(copy):
        copy.start()

    def pass_on(k, h):
        @pl.when(zz - k >= 0)
        def _():
            spread(zz - k, yy, h, 2, (zz, 1 - yy)).wait_recv()
            forward(zz - k, h, start)

        @pl.when(zz + k < Z)
        def _():
            spread(zz + k, yy, h, 2, (zz, 1 - yy)).wait_recv()
            forward(zz + k, h, start)

    def arrive(m):
        z = nth(m)
        a_u = dh = 0.0
        for h in range(2):
            spread(z, 1 - yy, h, 2, (zz, 1 - yy)).wait_recv()
            both = buf[z, :, h].astype(F32).reshape(2 * n_dp * W, 2, CAP, half)
            x = both[:, 0].reshape(2 * rows, half).astype(BF16)
            g = both[:, 1].reshape(2 * rows, half).astype(BF16)
            cut = slice(h * half, (h + 1) * half)
            xall[z, :, cut] = x
            a_u = a_u + jnp.dot(x, gu_ref[cut], preferred_element_type=F32)
            dh = dh + jnp.dot(g, downt[cut], preferred_element_type=F32)
        a_u = a_u.reshape(2, n_dp, W * CAP, 2 * hidden)
        dh = dh.reshape(2, n_dp, W * CAP, hidden)
        part[z, :, :, : 2 * hidden] = jnp.concatenate([a_u[0], a_u[1]], axis=1).astype(BF16)
        part[z, :, :, 2 * hidden :] = jnp.concatenate([dh[0], dh[1]], axis=1).astype(BF16)
        for k in range(1, n_dp):
            reduce_copy(z, (me_d + k) % n_dp, me_d).start()

    def activate(m):
        z = nth(m)
        total = part[z, me_d].astype(F32)
        for k in range(1, n_dp):
            d = (me_d + k) % n_dp
            reduce_copy(z, d, d).wait_recv()
            total = total + prcv[z, d].astype(F32)
        pre = total[:, :hidden]
        up_part = total[:, hidden : 2 * hidden]
        dh = total[:, 2 * hidden :]
        sig = jax.nn.sigmoid(pre)
        dgate = dh * up_part * sig * (1.0 + pre * (1.0 - sig))
        dup = dh * (pre * sig)
        dgrcv[z, me_d] = jnp.concatenate(
            [dgate.reshape(2 * W, CAP, hidden), dup.reshape(2 * W, CAP, hidden)], axis=1
        ).astype(BF16)
        for k in range(1, n_dp):
            share_copy(z, (me_d + k) % n_dp, me_d).start()

    def give_back(m):
        z = nth(m)
        for k in range(1, n_dp):
            d = (me_d + k) % n_dp
            share_copy(z, d, d).wait_recv()
        both = dgrcv[z].astype(F32).reshape(n_dp, 2, W, 2, CAP, hidden)
        dgate = jnp.concatenate([both[:, y, :, 0].reshape(rows, hidden) for y in range(2)], axis=0)
        dup = jnp.concatenate([both[:, y, :, 1].reshape(rows, hidden) for y in range(2)], axis=0)
        dgu = jnp.concatenate([dgate, dup], axis=1).astype(BF16)
        dguall[z] = dgu
        dx = jnp.dot(dgu, gut[...], preferred_element_type=F32).astype(BF16)
        dxs[z] = dx.reshape(2, rows, cols)
        return_copy(z, 1 - yy, zz, yy).start()

        @pl.when(m > 0)
        def _():
            return_copy(z, yy, zz, yy).start()

    def step(m, carry):
        @pl.when(m < Z)
        def _():
            pass_on(m + 1, 1)
            arrive(m)
            pass_on(m + 2, 0)

        @pl.when((m >= 1) & (m < Z + 1))
        def _():
            activate(m - 1)

        @pl.when(m >= 2)
        def _():
            give_back(m - 2)

        return carry

    for h in range(2):
        for k in range(1, n_same):
            pick_arrival(h, *same(k)).wait_recv()
        forward(zz, h, start)
    gut[...] = gu_ref[...].T
    pass_on(1, 0)
    lax.fori_loop(0, Z + 2, step, 0)

    gw_ref[0] = lax.dot_general(
        xall[...].reshape(S * rows, cols), dguall[...].reshape(S * rows, 2 * hidden), TN,
        preferred_element_type=F32,
    ).astype(BF16)

    total = dxs[zz, yy].astype(F32)
    for k in range(1, S):
        z, y = other(k)
        return_copy(z, y, z, y).wait_recv()
        total = total + ret[z, y].astype(F32)
    total = total.reshape(n_dp, W, CAP, cols)
    back[...] = jnp.concatenate(
        [total[..., : cols // 2], total[..., cols // 2 :]], axis=2
    ).astype(BF16)

    def fin_copy(d, w, owner_d, owner_w):
        return pltpu.make_async_remote_copy(
            src_ref=back.at[d, w], dst_ref=fin.at[owner_d, owner_w],
            send_sem=s_fin.at[d, w], recv_sem=r_fin.at[owner_d, owner_w],
            device_id=(d, w * S + me_s), device_id_type=MESH,
        )

    for k in range(1, n_same):
        d, w = same(k)
        fin_copy(d, w, me_d, me_w).start()
    fin[me_d, me_w] = back[me_d, me_w]

    for k in range(1, n_same):
        for h in range(2):
            pick_copy(h, *same(k)).wait_send()
    for k in range(1, S):
        z, y = other(k)
        return_copy(z, y, zz, yy).wait_send()

    def wait_send(copy):
        copy.wait_send()

    def drain(z, carry):
        for h in range(2):
            forward(z, h, wait_send)
        for k in range(1, n_dp):
            d = (me_d + k) % n_dp
            reduce_copy(z, d, me_d).wait_send()
            share_copy(z, d, me_d).wait_send()
        return carry

    lax.fori_loop(0, Z, drain, 0)
    for k in range(1, n_same):
        d, w = same(k)
        fin_copy(d, w, d, w).wait_recv()
        fin_copy(d, w, me_d, me_w).wait_send()
    fin_ref[...] = fin[...]


def place_rows(fin_hbm, slot_hbm, gw_hbm, gx_ref, gw_ref, fin_ref, slot_ref, sems):
    n_dp, W, _, half = fin_ref.shape
    tokens = gx_ref.shape[0]
    copies = [
        pltpu.make_async_copy(slot_hbm, slot_ref, sems.at[0]),
        pltpu.make_async_copy(fin_hbm, fin_ref, sems.at[1]),
        pltpu.make_async_copy(gw_hbm, gw_ref, sems.at[2]),
    ]
    for copy in copies:
        copy.start()
    copies[0].wait()
    copies[1].wait()
    place = lax.broadcasted_iota(jnp.int32, (2 * CAP, tokens), 0)
    for h in range(2):
        hits = []
        for e in range(W):
            hit = (slot_ref[e : e + 1, :] == place - h * CAP) & (place >= h * CAP)
            hits.append(jnp.where(hit, 1.0, 0.0).T.astype(BF16))
        for d in range(n_dp):
            out = jnp.dot(hits[0], fin_ref[d, 0], preferred_element_type=F32)
            for e in range(1, W):
                out = out + jnp.dot(hits[e], fin_ref[d, e], preferred_element_type=F32)
            at = (2 * d + h) * half
            gx_ref[:, at : at + half] = out.astype(BF16)
    copies[2].wait()


def on_device(n_dp, tokens, output_gradient, slot, gate_weight, gate_up_weight, down_weight):
    W = slot.shape[1]
    S = GROUP
    Z = S // 2
    _, cols, wide = gate_up_weight.shape
    hidden = wide // 2
    rows = n_dp * W * CAP
    vmem = pl.BlockSpec(memory_space=pltpu.VMEM)
    dma = pltpu.SemaphoreType.DMA
    slot_row = slot.T
    fin, grad_gate_up = pl.pallas_call(
        functools.partial(kernel, n_dp, W),
        out_shape=(
            jax.ShapeDtypeStruct((n_dp, W, 2 * CAP, cols // 2), BF16),
            jax.ShapeDtypeStruct(gate_up_weight.shape, BF16),
        ),
        in_specs=[vmem] * 6,
        out_specs=(vmem, vmem),
        scratch_shapes=[
            pltpu.VMEM((2, n_dp, W, 2 * CAP, cols // 2), BF16),
            pltpu.VMEM((Z, 2, 2, n_dp, W, 2 * CAP, cols // 2), BF16),
            pltpu.VMEM((Z, 2 * rows, cols), BF16),
            pltpu.VMEM((Z, n_dp, 2 * W * CAP, 3 * hidden), BF16),
            pltpu.VMEM((Z, n_dp, 2 * W * CAP, 3 * hidden), BF16),
            pltpu.VMEM((Z, n_dp, 2 * W, 2 * CAP, hidden), BF16),
            pltpu.VMEM((Z, 2 * rows, wide), BF16),
            pltpu.VMEM((Z, 2, rows, cols), BF16),
            pltpu.VMEM((Z, 2, rows, cols), BF16),
            pltpu.VMEM((n_dp, W, 2 * CAP, cols // 2), BF16),
            pltpu.VMEM((n_dp, W, 2 * CAP, cols // 2), BF16),
            pltpu.VMEM((wide, cols), BF16),
            pltpu.VMEM((cols, hidden), BF16),
            dma((2, n_dp, W)), dma((2, n_dp, W)),
            dma((Z, 2, 3)), dma((Z, 2, 2)),
            dma((Z, n_dp)), dma((Z, n_dp)),
            dma((Z, n_dp)), dma((Z, n_dp)),
            dma((Z, 2)), dma((Z, 2)),
            dma((n_dp, W)), dma((n_dp, W)),
        ],
        compiler_params=pltpu.CompilerParams(
            collective_id=0, has_side_effects=True, vmem_limit_bytes=58 * 1024 * 1024
        ),
        cost_estimate=pl.CostEstimate(
            flops=14 * S * rows * cols * hidden,
            bytes_accessed=4 * tokens.size + 4 * gate_up_weight.size, transcendentals=0,
        ),
        name="routed_backward",
    )(tokens, output_gradient, slot_row, gate_weight.T, gate_up_weight[0], down_weight[0])
    anywhere = pl.BlockSpec(memory_space=pl.ANY)
    return pl.pallas_call(
        place_rows,
        out_shape=(
            jax.ShapeDtypeStruct(tokens.shape, BF16),
            jax.ShapeDtypeStruct(gate_up_weight.shape, BF16),
        ),
        in_specs=[anywhere] * 3,
        out_specs=(vmem, vmem),
        scratch_shapes=[
            pltpu.VMEM(fin.shape, BF16),
            pltpu.VMEM(slot_row.shape, jnp.int32),
            dma((3,)),
        ],
        compiler_params=pltpu.CompilerParams(vmem_limit_bytes=58 * 1024 * 1024),
        name="place_rows",
    )(fin, slot_row, grad_gate_up)


def solution(mesh):
    in_specs = (
        P(("dp", "expert"), None),
        P(("dp", "expert"), None),
        P(("dp", "expert"), None),
        P(("dp", "expert"), None),
        P("expert", "dp", None),
        P("expert", None, "dp"),
    )
    out_specs = (P(("dp", "expert"), None), P("expert", "dp", None))
    return jax.shard_map(
        functools.partial(on_device, mesh.shape["dp"]),
        mesh=mesh, in_specs=in_specs, out_specs=out_specs, check_vma=False,
    )
```

```python
import functools

import jax
import jax.numpy as jnp
from jax import lax
from jax.experimental import pallas as pl
from jax.experimental.pallas import tpu as pltpu
from jax.sharding import PartitionSpec as P

GROUP = 8
CAP = 8
MESH = pl.DeviceIdType.MESH
F32 = jnp.float32
BF16 = jnp.bfloat16
NT = (((1,), (1,)), ((), ()))
TN = (((0,), (0,)), ((), ()))


def kernel(
    n_dp, windows,
    tok_ref, dy_ref, slot_ref, gate_ref, gu_ref, down_ref,
    fin_ref, gw_ref,
    pick, buf, xall, part, prcv, dgrcv, dguall, dxs, across, sums, ret, back, fin, gut, downt,
    s_pick, r_pick, s_ag, r_ag, s_rs, r_rs, s_dg, r_dg, s_cross, r_cross, s_ret, r_ret, s_fin, r_fin,
):
    S = GROUP
    Z = S // 2
    W = windows
    n_same = n_dp * W
    tokens, width = tok_ref.shape
    cols = width // n_dp
    half = cols // 2
    hidden = down_ref.shape[0]
    rows = n_dp * W * CAP
    me_d = lax.axis_index("dp")
    me_x = lax.axis_index("expert")
    me_w = me_x // S
    me_s = me_x % S
    zz = me_s // 2
    yy = me_s % 2

    def member(z, y):
        return (me_d, me_w * S + z * 2 + y)

    barrier = pltpu.get_barrier_semaphore()

    def same(k):
        flat = (me_d * W + me_w + k) % n_same
        return flat // W, flat % W

    def other(k):
        s = (me_s + k) % S
        return s // 2, s % 2

    for k in range(1, n_same):
        d, w = same(k)
        pl.semaphore_signal(barrier, inc=1, device_id=(d, w * S + me_s), device_id_type=MESH)
    for k in range(1, S):
        pl.semaphore_signal(barrier, inc=1, device_id=member(*other(k)), device_id_type=MESH)

    def pick_copy(h, d, w):
        return pltpu.make_async_remote_copy(
            src_ref=pick.at[h, d, w], dst_ref=buf.at[zz, yy, h, me_d, me_w],
            send_sem=s_pick.at[h, d, w], recv_sem=r_pick.at[h, me_d, me_w],
            device_id=(d, w * S + me_s), device_id_type=MESH,
        )

    def pick_arrival(h, d, w):
        return pltpu.make_async_remote_copy(
            src_ref=pick.at[h, d, w], dst_ref=buf.at[zz, yy, h, d, w],
            send_sem=s_pick.at[h, d, w], recv_sem=r_pick.at[h, d, w],
            device_id=(d, w * S + me_s), device_id_type=MESH,
        )

    place = lax.broadcasted_iota(jnp.int32, (CAP, tokens), 0)
    sels, weights = [], []
    for e in range(W):
        hit = slot_ref[e : e + 1, :] == place
        sels.append(jnp.where(hit, 1.0, 0.0).astype(BF16))
        weights.append(
            jnp.sum(jnp.where(hit, gate_ref[e : e + 1, :], 0.0), axis=1, keepdims=True)
        )
    for h in range(2):
        for e in range(W):
            for d in range(n_dp):
                cut = slice(d * cols + h * half, d * cols + (h + 1) * half)
                x = jnp.dot(sels[e], tok_ref[:, cut], preferred_element_type=F32)
                g = jnp.dot(sels[e], dy_ref[:, cut], preferred_element_type=F32) * weights[e]
                pick[h, d, e] = jnp.concatenate([x, g], axis=0).astype(BF16)
        if h == 0:
            pl.semaphore_wait(barrier, n_same - 1 + S - 1)
        for k in range(1, n_same):
            pick_copy(h, *same(k)).start()
        buf[zz, yy, h, me_d, me_w] = pick[h, me_d, me_w]
    downt[...] = down_ref[...].T

    def spread(z, y, h, way, target):
        return pltpu.make_async_remote_copy(
            src_ref=buf.at[z, y, h], dst_ref=buf.at[z, y, h],
            send_sem=s_ag.at[z, h, way], recv_sem=r_ag.at[z, y, h],
            device_id=member(*target), device_id_type=MESH,
        )

    def reduce_copy(z, d, owner):
        return pltpu.make_async_remote_copy(
            src_ref=part.at[z, d], dst_ref=prcv.at[z, owner],
            send_sem=s_rs.at[z, d], recv_sem=r_rs.at[z, owner],
            device_id=(d, me_x), device_id_type=MESH,
        )

    def share_copy(z, d, owner):
        return pltpu.make_async_remote_copy(
            src_ref=dgrcv.at[z, me_d], dst_ref=dgrcv.at[z, owner],
            send_sem=s_dg.at[z, d], recv_sem=r_dg.at[z, owner],
            device_id=(d, me_x), device_id_type=MESH,
        )

    def cross_copy(z):
        return pltpu.make_async_remote_copy(
            src_ref=dxs.at[z, 1 - yy], dst_ref=across.at[z],
            send_sem=s_cross.at[z], recv_sem=r_cross.at[z],
            device_id=member(zz, 1 - yy), device_id_type=MESH,
        )

    def return_copy(z, owner):
        return pltpu.make_async_remote_copy(
            src_ref=sums.at[z], dst_ref=ret.at[owner],
            send_sem=s_ret.at[z], recv_sem=r_ret.at[owner],
            device_id=member(z, yy), device_id_type=MESH,
        )

    near = jnp.minimum(zz, Z - 1 - zz)

    def nth(m):
        alternating = ((m + 1) // 2) * (1 - 2 * (m % 2))
        far = m - near
        beyond = jnp.where(zz > Z - 1 - zz, -far, far)
        return zz + jnp.where(m <= 2 * near, alternating, beyond)

    def forward(z, h, act):
        @pl.when((z <= zz) & (zz + 1 < Z))
        def _():
            act(spread(z, yy, h, 0, (zz + 1, yy)))

        @pl.when((z >= zz) & (zz >= 1))
        def _():
            act(spread(z, yy, h, 1, (zz - 1, yy)))

        act(spread(z, yy, h, 2, (zz, 1 - yy)))

    def start(copy):
        copy.start()

    def pass_on(k, h):
        @pl.when(zz - k >= 0)
        def _():
            spread(zz - k, yy, h, 2, (zz, 1 - yy)).wait_recv()
            forward(zz - k, h, start)

        @pl.when(zz + k < Z)
        def _():
            spread(zz + k, yy, h, 2, (zz, 1 - yy)).wait_recv()
            forward(zz + k, h, start)

    def arrive(m):
        z = nth(m)
        a_u = dh = 0.0
        for h in range(2):
            spread(z, 1 - yy, h, 2, (zz, 1 - yy)).wait_recv()
            both = buf[z, :, h].astype(F32).reshape(2 * n_dp * W, 2, CAP, half)
            x = both[:, 0].reshape(2 * rows, half).astype(BF16)
            g = both[:, 1].reshape(2 * rows, half).astype(BF16)
            cut = slice(h * half, (h + 1) * half)
            xall[z, :, cut] = x
            a_u = a_u + jnp.dot(x, gu_ref[cut], preferred_element_type=F32)
            dh = dh + jnp.dot(g, downt[cut], preferred_element_type=F32)
        a_u = a_u.reshape(2, n_dp, W * CAP, 2 * hidden)
        dh = dh.reshape(2, n_dp, W * CAP, hidden)
        part[z, :, :, : 2 * hidden] = jnp.concatenate([a_u[0], a_u[1]], axis=1).astype(BF16)
        part[z, :, :, 2 * hidden :] = jnp.concatenate([dh[0], dh[1]], axis=1).astype(BF16)
        for k in range(1, n_dp):
            reduce_copy(z, (me_d + k) % n_dp, me_d).start()

    def activate(m):
        z = nth(m)
        total = part[z, me_d].astype(F32)
        for k in range(1, n_dp):
            d = (me_d + k) % n_dp
            reduce_copy(z, d, d).wait_recv()
            total = total + prcv[z, d].astype(F32)
        pre = total[:, :hidden]
        up_part = total[:, hidden : 2 * hidden]
        dh = total[:, 2 * hidden :]
        sig = jax.nn.sigmoid(pre)
        dgate = dh * up_part * sig * (1.0 + pre * (1.0 - sig))
        dup = dh * (pre * sig)
        dgrcv[z, me_d] = jnp.concatenate(
            [dgate.reshape(2 * W, CAP, hidden), dup.reshape(2 * W, CAP, hidden)], axis=1
        ).astype(BF16)
        for k in range(1, n_dp):
            share_copy(z, (me_d + k) % n_dp, me_d).start()

    def give_back(m):
        z = nth(m)
        for k in range(1, n_dp):
            d = (me_d + k) % n_dp
            share_copy(z, d, d).wait_recv()
        both = dgrcv[z].astype(F32).reshape(n_dp, 2, W, 2, CAP, hidden)
        dgate = jnp.concatenate([both[:, y, :, 0].reshape(rows, hidden) for y in range(2)], axis=0)
        dup = jnp.concatenate([both[:, y, :, 1].reshape(rows, hidden) for y in range(2)], axis=0)
        dgu = jnp.concatenate([dgate, dup], axis=1).astype(BF16)
        dguall[z] = dgu
        dx = jnp.dot(dgu, gut[...], preferred_element_type=F32).astype(BF16)
        dxs[z] = dx.reshape(2, rows, cols)
        cross_copy(z).start()

    def combine(m):
        z = nth(m)
        cross_copy(z).wait_recv()
        sums[z] = (dxs[z, yy].astype(F32) + across[z].astype(F32)).astype(BF16)

        @pl.when(m > 0)
        def _():
            return_copy(z, zz).start()

    def step(m, carry):
        @pl.when(m < Z)
        def _():
            pass_on(m + 1, 1)
            arrive(m)
            pass_on(m + 2, 0)

        @pl.when((m >= 1) & (m < Z + 1))
        def _():
            activate(m - 1)

        @pl.when(m >= 2)
        def _():
            give_back(m - 2)

        @pl.when(m >= 3)
        def _():
            combine(m - 3)

        return carry

    for h in range(2):
        for k in range(1, n_same):
            pick_arrival(h, *same(k)).wait_recv()
        forward(zz, h, start)
    gut[...] = gu_ref[...].T
    pass_on(1, 0)
    lax.fori_loop(0, Z + 2, step, 0)

    def weight_gradient(h):
        cut = slice(h * half, (h + 1) * half)
        gw_ref[0, cut] = lax.dot_general(
            xall[:, :, cut].reshape(S * rows, half), dguall[...].reshape(S * rows, 2 * hidden), TN,
            preferred_element_type=F32,
        ).astype(BF16)

    weight_gradient(0)
    combine(Z - 1)
    weight_gradient(1)

    total = sums[zz].astype(F32)
    for k in range(1, Z):
        z = (zz + k) % Z
        return_copy(z, z).wait_recv()
        total = total + ret[z].astype(F32)
    total = total.reshape(n_dp, W, CAP, cols)
    back[...] = jnp.concatenate(
        [total[..., : cols // 2], total[..., cols // 2 :]], axis=2
    ).astype(BF16)

    def fin_copy(d, w, owner_d, owner_w):
        return pltpu.make_async_remote_copy(
            src_ref=back.at[d, w], dst_ref=fin.at[owner_d, owner_w],
            send_sem=s_fin.at[d, w], recv_sem=r_fin.at[owner_d, owner_w],
            device_id=(d, w * S + me_s), device_id_type=MESH,
        )

    for k in range(1, n_same):
        d, w = same(k)
        fin_copy(d, w, me_d, me_w).start()
    fin[me_d, me_w] = back[me_d, me_w]

    for k in range(1, n_same):
        for h in range(2):
            pick_copy(h, *same(k)).wait_send()
    for k in range(1, Z):
        return_copy((zz + k) % Z, zz).wait_send()

    def wait_send(copy):
        copy.wait_send()

    def drain(z, carry):
        for h in range(2):
            forward(z, h, wait_send)
        cross_copy(z).wait_send()
        for k in range(1, n_dp):
            d = (me_d + k) % n_dp
            reduce_copy(z, d, me_d).wait_send()
            share_copy(z, d, me_d).wait_send()
        return carry

    lax.fori_loop(0, Z, drain, 0)
    for k in range(1, n_same):
        d, w = same(k)
        fin_copy(d, w, d, w).wait_recv()
        fin_copy(d, w, me_d, me_w).wait_send()
    fin_ref[...] = fin[...]


def place_rows(fin_hbm, slot_hbm, gw_hbm, gx_ref, gw_ref, fin_ref, slot_ref, sems):
    n_dp, W, _, half = fin_ref.shape
    tokens = gx_ref.shape[0]
    copies = [
        pltpu.make_async_copy(slot_hbm, slot_ref, sems.at[0]),
        pltpu.make_async_copy(fin_hbm, fin_ref, sems.at[1]),
        pltpu.make_async_copy(gw_hbm, gw_ref, sems.at[2]),
    ]
    for copy in copies:
        copy.start()
    copies[0].wait()
    copies[1].wait()
    place = lax.broadcasted_iota(jnp.int32, (2 * CAP, tokens), 0)
    for h in range(2):
        hits = []
        for e in range(W):
            hit = (slot_ref[e : e + 1, :] == place - h * CAP) & (place >= h * CAP)
            hits.append(jnp.where(hit, 1.0, 0.0).T.astype(BF16))
        for d in range(n_dp):
            out = jnp.dot(hits[0], fin_ref[d, 0], preferred_element_type=F32)
            for e in range(1, W):
                out = out + jnp.dot(hits[e], fin_ref[d, e], preferred_element_type=F32)
            at = (2 * d + h) * half
            gx_ref[:, at : at + half] = out.astype(BF16)
    copies[2].wait()


def on_device(n_dp, tokens, output_gradient, slot, gate_weight, gate_up_weight, down_weight):
    W = slot.shape[1]
    S = GROUP
    Z = S // 2
    _, cols, wide = gate_up_weight.shape
    hidden = wide // 2
    rows = n_dp * W * CAP
    vmem = pl.BlockSpec(memory_space=pltpu.VMEM)
    dma = pltpu.SemaphoreType.DMA
    slot_row = slot.T
    fin, grad_gate_up = pl.pallas_call(
        functools.partial(kernel, n_dp, W),
        out_shape=(
            jax.ShapeDtypeStruct((n_dp, W, 2 * CAP, cols // 2), BF16),
            jax.ShapeDtypeStruct(gate_up_weight.shape, BF16),
        ),
        in_specs=[vmem] * 6,
        out_specs=(vmem, vmem),
        scratch_shapes=[
            pltpu.VMEM((2, n_dp, W, 2 * CAP, cols // 2), BF16),
            pltpu.VMEM((Z, 2, 2, n_dp, W, 2 * CAP, cols // 2), BF16),
            pltpu.VMEM((Z, 2 * rows, cols), BF16),
            pltpu.VMEM((Z, n_dp, 2 * W * CAP, 3 * hidden), BF16),
            pltpu.VMEM((Z, n_dp, 2 * W * CAP, 3 * hidden), BF16),
            pltpu.VMEM((Z, n_dp, 2 * W, 2 * CAP, hidden), BF16),
            pltpu.VMEM((Z, 2 * rows, wide), BF16),
            pltpu.VMEM((Z, 2, rows, cols), BF16),
            pltpu.VMEM((Z, rows, cols), BF16),
            pltpu.VMEM((Z, rows, cols), BF16),
            pltpu.VMEM((Z, rows, cols), BF16),
            pltpu.VMEM((n_dp, W, 2 * CAP, cols // 2), BF16),
            pltpu.VMEM((n_dp, W, 2 * CAP, cols // 2), BF16),
            pltpu.VMEM((wide, cols), BF16),
            pltpu.VMEM((cols, hidden), BF16),
            dma((2, n_dp, W)), dma((2, n_dp, W)),
            dma((Z, 2, 3)), dma((Z, 2, 2)),
            dma((Z, n_dp)), dma((Z, n_dp)),
            dma((Z, n_dp)), dma((Z, n_dp)),
            dma((Z,)), dma((Z,)),
            dma((Z,)), dma((Z,)),
            dma((n_dp, W)), dma((n_dp, W)),
        ],
        compiler_params=pltpu.CompilerParams(
            collective_id=0, has_side_effects=True, vmem_limit_bytes=58 * 1024 * 1024
        ),
        cost_estimate=pl.CostEstimate(
            flops=14 * S * rows * cols * hidden,
            bytes_accessed=4 * tokens.size + 4 * gate_up_weight.size, transcendentals=0,
        ),
        name="routed_backward",
    )(tokens, output_gradient, slot_row, gate_weight.T, gate_up_weight[0], down_weight[0])
    anywhere = pl.BlockSpec(memory_space=pl.ANY)
    return pl.pallas_call(
        place_rows,
        out_shape=(
            jax.ShapeDtypeStruct(tokens.shape, BF16),
            jax.ShapeDtypeStruct(gate_up_weight.shape, BF16),
        ),
        in_specs=[anywhere] * 3,
        out_specs=(vmem, vmem),
        scratch_shapes=[
            pltpu.VMEM(fin.shape, BF16),
            pltpu.VMEM(slot_row.shape, jnp.int32),
            dma((3,)),
        ],
        compiler_params=pltpu.CompilerParams(vmem_limit_bytes=58 * 1024 * 1024),
        name="place_rows",
    )(fin, slot_row, grad_gate_up)


def solution(mesh):
    in_specs = (
        P(("dp", "expert"), None),
        P(("dp", "expert"), None),
        P(("dp", "expert"), None),
        P(("dp", "expert"), None),
        P("expert", "dp", None),
        P("expert", None, "dp"),
    )
    out_specs = (P(("dp", "expert"), None), P("expert", "dp", None))
    return jax.shard_map(
        functools.partial(on_device, mesh.shape["dp"]),
        mesh=mesh, in_specs=in_specs, out_specs=out_specs, check_vma=False,
    )
```

```python
import functools

import jax
import jax.numpy as jnp
from jax import lax
from jax.experimental import pallas as pl
from jax.experimental.pallas import tpu as pltpu
from jax.sharding import PartitionSpec as P

GROUP = 8
CAP = 8
MESH = pl.DeviceIdType.MESH
F32 = jnp.float32
BF16 = jnp.bfloat16
NT = (((1,), (1,)), ((), ()))
TN = (((0,), (0,)), ((), ()))


def kernel(
    n_dp, windows,
    tok_hbm, dy_hbm, slot_hbm, gate_hbm, gu_hbm, down_hbm,
    fin_ref, gw_hbm,
    tok_ref, dy_ref, slot_ref, gate_ref, gu_ref, down_ref, gw_ref,
    pick, buf, xall, part, prcv, dgrcv, dguall, dxs, across, sums, ret, gut, downt,
    s_in, s_out,
    s_pick, r_pick, s_ag, r_ag, s_rs, r_rs, s_dg, r_dg, s_cross, r_cross, s_ret, r_ret,
):
    S = GROUP
    Z = S // 2
    W = windows
    n_same = n_dp * W
    tokens, width = tok_ref.shape
    cols = width // n_dp
    half = cols // 2
    hidden = down_ref.shape[0]
    rows = n_dp * W * CAP
    me_d = lax.axis_index("dp")
    me_x = lax.axis_index("expert")
    me_w = me_x // S
    me_s = me_x % S
    zz = me_s // 2
    yy = me_s % 2

    def member(z, y):
        return (me_d, me_w * S + z * 2 + y)

    small = [
        pltpu.make_async_copy(slot_hbm, slot_ref, s_in.at[0]),
        pltpu.make_async_copy(gate_hbm, gate_ref, s_in.at[1]),
    ]
    big = []
    for d in range(n_dp):
        cut = pl.ds(d * cols, cols)
        at = 4 + 2 * d
        big.append(pltpu.make_async_copy(tok_hbm.at[:, cut], tok_ref.at[:, cut], s_in.at[at]))
        big.append(pltpu.make_async_copy(dy_hbm.at[:, cut], dy_ref.at[:, cut], s_in.at[at + 1]))
    down_in = pltpu.make_async_copy(down_hbm, down_ref, s_in.at[2])
    gu_in = pltpu.make_async_copy(gu_hbm, gu_ref, s_in.at[3])
    for copy in small + big + [down_in, gu_in]:
        copy.start()

    barrier = pltpu.get_barrier_semaphore()
    n_peer = n_same * Z
    me_flat = (me_d * W + me_w) * Z + zz

    def greet(k, carry):
        flat = (me_flat + k) % n_peer
        owner = flat // Z
        target = (owner // W, (owner % W) * S + (flat % Z) * 2 + yy)
        pl.semaphore_signal(barrier, inc=1, device_id=target, device_id_type=MESH)
        return carry

    lax.fori_loop(1, n_peer, greet, 0)
    pl.semaphore_signal(barrier, inc=1, device_id=member(zz, 1 - yy), device_id_type=MESH)

    def same(k):
        flat = (me_d * W + me_w + k) % n_same
        return flat // W, flat % W

    def pick_copy(h, d, w):
        return pltpu.make_async_remote_copy(
            src_ref=pick.at[h, d, w], dst_ref=buf.at[zz, yy, h, me_d, me_w],
            send_sem=s_pick.at[h, d, w], recv_sem=r_pick.at[h, me_d, me_w],
            device_id=(d, w * S + me_s), device_id_type=MESH,
        )

    def pick_arrival(h, d, w):
        return pltpu.make_async_remote_copy(
            src_ref=pick.at[h, d, w], dst_ref=buf.at[zz, yy, h, d, w],
            send_sem=s_pick.at[h, d, w], recv_sem=r_pick.at[h, d, w],
            device_id=(d, w * S + me_s), device_id_type=MESH,
        )

    for copy in small:
        copy.wait()
    place = lax.broadcasted_iota(jnp.int32, (CAP, tokens), 0)
    sels, weights = [], []
    for e in range(W):
        hit = slot_ref[e : e + 1, :] == place
        sels.append(jnp.where(hit, 1.0, 0.0).astype(BF16))
        weights.append(
            jnp.sum(jnp.where(hit, gate_ref[e : e + 1, :], 0.0), axis=1, keepdims=True)
        )
    for copy in big:
        copy.wait()
    for h in range(2):
        for e in range(W):
            for d in range(n_dp):
                cut = slice(d * cols + h * half, d * cols + (h + 1) * half)
                x = jnp.dot(sels[e], tok_ref[:, cut], preferred_element_type=F32)
                g = jnp.dot(sels[e], dy_ref[:, cut], preferred_element_type=F32) * weights[e]
                pick[h, d, e] = jnp.concatenate([x, g], axis=0).astype(BF16)
        if h == 0:
            pl.semaphore_wait(barrier, n_peer)
        for k in range(1, n_same):
            pick_copy(h, *same(k)).start()
        buf[zz, yy, h, me_d, me_w] = pick[h, me_d, me_w]
    down_in.wait()
    downt[...] = down_ref[...].T

    def spread(z, y, h, way, target):
        return pltpu.make_async_remote_copy(
            src_ref=buf.at[z, y, h], dst_ref=buf.at[z, y, h],
            send_sem=s_ag.at[z, h, way], recv_sem=r_ag.at[z, y, h],
            device_id=member(*target), device_id_type=MESH,
        )

    def reduce_copy(z, d, owner):
        return pltpu.make_async_remote_copy(
            src_ref=part.at[z, d], dst_ref=prcv.at[z, owner],
            send_sem=s_rs.at[z, d], recv_sem=r_rs.at[z, owner],
            device_id=(d, me_x), device_id_type=MESH,
        )

    def share_copy(z, d, owner):
        return pltpu.make_async_remote_copy(
            src_ref=dgrcv.at[z, me_d], dst_ref=dgrcv.at[z, owner],
            send_sem=s_dg.at[z, d], recv_sem=r_dg.at[z, owner],
            device_id=(d, me_x), device_id_type=MESH,
        )

    def cross_copy(z):
        return pltpu.make_async_remote_copy(
            src_ref=dxs.at[z, 1 - yy], dst_ref=across.at[z],
            send_sem=s_cross.at[z], recv_sem=r_cross.at[z],
            device_id=member(zz, 1 - yy), device_id_type=MESH,
        )

    def return_copy(z, d, w, owner_z, owner_d, owner_w):
        return pltpu.make_async_remote_copy(
            src_ref=sums.at[z, d, w], dst_ref=ret.at[owner_z, owner_d, owner_w],
            send_sem=s_ret.at[z, d, w], recv_sem=r_ret.at[owner_z, owner_d, owner_w],
            device_id=(d, w * S + z * 2 + yy), device_id_type=MESH,
        )

    def returns(z, act):
        for k in range(1, n_same):
            d, w = same(k)
            act(return_copy(z, d, w, zz, me_d, me_w))

        @pl.when(z != zz)
        def _():
            act(return_copy(z, me_d, me_w, zz, me_d, me_w))

    near = jnp.minimum(zz, Z - 1 - zz)

    def nth(m):
        alternating = ((m + 1) // 2) * (1 - 2 * (m % 2))
        far = m - near
        beyond = jnp.where(zz > Z - 1 - zz, -far, far)
        return zz + jnp.where(m <= 2 * near, alternating, beyond)

    def forward(z, h, act):
        @pl.when((z <= zz) & (zz + 1 < Z))
        def _():
            act(spread(z, yy, h, 0, (zz + 1, yy)))

        @pl.when((z >= zz) & (zz >= 1))
        def _():
            act(spread(z, yy, h, 1, (zz - 1, yy)))

        act(spread(z, yy, h, 2, (zz, 1 - yy)))

    def start(copy):
        copy.start()

    def pass_on(k, h):
        @pl.when(zz - k >= 0)
        def _():
            spread(zz - k, yy, h, 2, (zz, 1 - yy)).wait_recv()
            forward(zz - k, h, start)

        @pl.when(zz + k < Z)
        def _():
            spread(zz + k, yy, h, 2, (zz, 1 - yy)).wait_recv()
            forward(zz + k, h, start)

    def arrive(m):
        z = nth(m)
        a_u = dh = 0.0
        for h in range(2):
            spread(z, 1 - yy, h, 2, (zz, 1 - yy)).wait_recv()
            both = buf[z, :, h].astype(F32).reshape(2 * n_dp * W, 2, CAP, half)
            x = both[:, 0].reshape(2 * rows, half).astype(BF16)
            g = both[:, 1].reshape(2 * rows, half).astype(BF16)
            cut = slice(h * half, (h + 1) * half)
            xall[z, :, cut] = x
            a_u = a_u + jnp.dot(x, gu_ref[cut], preferred_element_type=F32)
            dh = dh + jnp.dot(g, downt[cut], preferred_element_type=F32)
        a_u = a_u.reshape(2, n_dp, W * CAP, 2 * hidden)
        dh = dh.reshape(2, n_dp, W * CAP, hidden)
        part[z, :, :, : 2 * hidden] = jnp.concatenate([a_u[0], a_u[1]], axis=1).astype(BF16)
        part[z, :, :, 2 * hidden :] = jnp.concatenate([dh[0], dh[1]], axis=1).astype(BF16)
        for k in range(1, n_dp):
            reduce_copy(z, (me_d + k) % n_dp, me_d).start()

    def activate(m):
        z = nth(m)
        total = part[z, me_d].astype(F32)
        for k in range(1, n_dp):
            d = (me_d + k) % n_dp
            reduce_copy(z, d, d).wait_recv()
            total = total + prcv[z, d].astype(F32)
        pre = total[:, :hidden]
        up_part = total[:, hidden : 2 * hidden]
        dh = total[:, 2 * hidden :]
        sig = jax.nn.sigmoid(pre)
        dgate = dh * up_part * sig * (1.0 + pre * (1.0 - sig))
        dup = dh * (pre * sig)
        dgrcv[z, me_d] = jnp.concatenate(
            [dgate.reshape(2 * W, CAP, hidden), dup.reshape(2 * W, CAP, hidden)], axis=1
        ).astype(BF16)
        for k in range(1, n_dp):
            share_copy(z, (me_d + k) % n_dp, me_d).start()

    def give_back(m):
        z = nth(m)
        for k in range(1, n_dp):
            d = (me_d + k) % n_dp
            share_copy(z, d, d).wait_recv()
        both = dgrcv[z].astype(F32).reshape(n_dp, 2, W, 2, CAP, hidden)
        dgate = jnp.concatenate([both[:, y, :, 0].reshape(rows, hidden) for y in range(2)], axis=0)
        dup = jnp.concatenate([both[:, y, :, 1].reshape(rows, hidden) for y in range(2)], axis=0)
        dgu = jnp.concatenate([dgate, dup], axis=1).astype(BF16)
        dguall[z] = dgu
        dx = jnp.dot(dgu, gut[...], preferred_element_type=F32).astype(BF16)
        dxs[z] = dx.reshape(2, rows, cols)
        cross_copy(z).start()

    def combine(m):
        z = nth(m)
        cross_copy(z).wait_recv()
        both = dxs[z, yy].astype(F32) + across[z].astype(F32)
        both = both.reshape(n_dp, W, CAP, cols)
        sums[z] = jnp.concatenate([both[..., :half], both[..., half:]], axis=2).astype(BF16)
        returns(z, start)

    def step(m, carry):
        @pl.when(m < Z)
        def _():
            pass_on(m + 1, 1)
            arrive(m)
            pass_on(m + 2, 0)

        @pl.when((m >= 1) & (m < Z + 1))
        def _():
            activate(m - 1)

        @pl.when(m >= 2)
        def _():
            give_back(m - 2)

        @pl.when(m >= 3)
        def _():
            combine(m - 3)

        return carry

    for h in range(2):
        for k in range(1, n_same):
            pick_arrival(h, *same(k)).wait_recv()
        forward(zz, h, start)
    gu_in.wait()
    gut[...] = gu_ref[...].T
    pass_on(1, 0)
    lax.fori_loop(0, Z + 2, step, 0)

    def weight_gradient(h):
        cut = slice(h * half, (h + 1) * half)
        gw_ref[0, cut] = lax.dot_general(
            xall[:, :, cut].reshape(S * rows, half), dguall[...].reshape(S * rows, 2 * hidden), TN,
            preferred_element_type=F32,
        ).astype(BF16)

    def gradient_out(h):
        cut = pl.ds(h * half, half)
        return pltpu.make_async_copy(gw_ref.at[0, cut], gw_hbm.at[0, cut], s_out.at[h])

    weight_gradient(0)
    gradient_out(0).start()
    combine(Z - 1)
    weight_gradient(1)
    gradient_out(1).start()

    for k in range(1, n_same):
        for h in range(2):
            pick_copy(h, *same(k)).wait_send()

    def wait_send(copy):
        copy.wait_send()

    def drain(z, carry):
        for h in range(2):
            forward(z, h, wait_send)
        cross_copy(z).wait_send()
        for k in range(1, n_dp):
            d = (me_d + k) % n_dp
            reduce_copy(z, d, me_d).wait_send()
            share_copy(z, d, me_d).wait_send()
        returns(z, wait_send)
        return carry

    lax.fori_loop(0, Z, drain, 0)

    total = 0.0
    ret[zz, me_d, me_w] = sums[zz, me_d, me_w]
    for j in range(Z):
        z = (zz + j) % Z
        for k in range(1 if j == 0 else 0, n_same):
            d, w = same(k)
            return_copy(z, d, w, z, d, w).wait_recv()
        total = total + ret[z].astype(F32)
    fin_ref[...] = total.astype(BF16)
    gradient_out(0).wait()
    gradient_out(1).wait()


def place_rows(
    fin_hbm, slot_hbm, gw_in, gx_hbm, gw_hbm, fin_ref, slot_ref, gx_ref, gw_ref, s_in, s_out
):
    n_dp, W, _, half = fin_ref.shape
    tokens = gx_ref.shape[0]
    slot_copy = pltpu.make_async_copy(slot_hbm, slot_ref, s_in.at[0])
    fin_copy = pltpu.make_async_copy(fin_hbm, fin_ref, s_in.at[1])
    gw_copy = pltpu.make_async_copy(gw_in, gw_ref, s_in.at[2])
    for copy in (slot_copy, fin_copy, gw_copy):
        copy.start()
    gw_out = pltpu.make_async_copy(gw_ref, gw_hbm, s_in.at[3])
    outs = []
    slot_copy.wait()
    place = lax.broadcasted_iota(jnp.int32, (2 * CAP, tokens), 0)
    hits = []
    for h in range(2):
        for e in range(W):
            hit = (slot_ref[e : e + 1, :] == place - h * CAP) & (place >= h * CAP)
            hits.append(jnp.where(hit, 1.0, 0.0).T.astype(BF16))
    fin_copy.wait()
    for d in range(n_dp):
        for h in range(2):
            out = jnp.dot(hits[h * W], fin_ref[d, 0], preferred_element_type=F32)
            for e in range(1, W):
                out = out + jnp.dot(hits[h * W + e], fin_ref[d, e], preferred_element_type=F32)
            at = (2 * d + h) * half
            gx_ref[:, at : at + half] = out.astype(BF16)
        cut = pl.ds(2 * d * half, 2 * half)
        outs.append(pltpu.make_async_copy(gx_ref.at[:, cut], gx_hbm.at[:, cut], s_out.at[d]))
        outs[d].start()
        if d == 0:
            gw_copy.wait()
            gw_out.start()
    for copy in outs:
        copy.wait()
    gw_out.wait()


def on_device(n_dp, tokens, output_gradient, slot, gate_weight, gate_up_weight, down_weight):
    W = slot.shape[1]
    S = GROUP
    Z = S // 2
    _, cols, wide = gate_up_weight.shape
    hidden = wide // 2
    rows = n_dp * W * CAP
    vmem = pl.BlockSpec(memory_space=pltpu.VMEM)
    anywhere = pl.BlockSpec(memory_space=pl.ANY)
    dma = pltpu.SemaphoreType.DMA
    slot_row = slot.T
    fin, grad_gate_up = pl.pallas_call(
        functools.partial(kernel, n_dp, W),
        out_shape=(
            jax.ShapeDtypeStruct((n_dp, W, 2 * CAP, cols // 2), BF16),
            jax.ShapeDtypeStruct(gate_up_weight.shape, BF16),
        ),
        in_specs=[anywhere] * 6,
        out_specs=(vmem, anywhere),
        scratch_shapes=[
            pltpu.VMEM(tokens.shape, BF16),
            pltpu.VMEM(tokens.shape, BF16),
            pltpu.VMEM(slot_row.shape, jnp.int32),
            pltpu.VMEM(slot_row.shape, F32),
            pltpu.VMEM((cols, wide), BF16),
            pltpu.VMEM((hidden, cols), BF16),
            pltpu.VMEM((1, cols, wide), BF16),
            pltpu.VMEM((2, n_dp, W, 2 * CAP, cols // 2), BF16),
            pltpu.VMEM((Z, 2, 2, n_dp, W, 2 * CAP, cols // 2), BF16),
            pltpu.VMEM((Z, 2 * rows, cols), BF16),
            pltpu.VMEM((Z, n_dp, 2 * W * CAP, 3 * hidden), BF16),
            pltpu.VMEM((Z, n_dp, 2 * W * CAP, 3 * hidden), BF16),
            pltpu.VMEM((Z, n_dp, 2 * W, 2 * CAP, hidden), BF16),
            pltpu.VMEM((Z, 2 * rows, wide), BF16),
            pltpu.VMEM((Z, 2, rows, cols), BF16),
            pltpu.VMEM((Z, rows, cols), BF16),
            pltpu.VMEM((Z, n_dp, W, 2 * CAP, cols // 2), BF16),
            pltpu.VMEM((Z, n_dp, W, 2 * CAP, cols // 2), BF16),
            pltpu.VMEM((wide, cols), BF16),
            pltpu.VMEM((cols, hidden), BF16),
            dma((4 + 2 * n_dp,)), dma((2,)),
            dma((2, n_dp, W)), dma((2, n_dp, W)),
            dma((Z, 2, 3)), dma((Z, 2, 2)),
            dma((Z, n_dp)), dma((Z, n_dp)),
            dma((Z, n_dp)), dma((Z, n_dp)),
            dma((Z,)), dma((Z,)),
            dma((Z, n_dp, W)), dma((Z, n_dp, W)),
        ],
        compiler_params=pltpu.CompilerParams(
            collective_id=0, has_side_effects=True, vmem_limit_bytes=58 * 1024 * 1024
        ),
        cost_estimate=pl.CostEstimate(
            flops=14 * S * rows * cols * hidden,
            bytes_accessed=4 * tokens.size + 4 * gate_up_weight.size, transcendentals=0,
        ),
        name="routed_backward",
    )(tokens, output_gradient, slot_row, gate_weight.T, gate_up_weight[0], down_weight[0])
    return pl.pallas_call(
        place_rows,
        out_shape=(
            jax.ShapeDtypeStruct(tokens.shape, BF16),
            jax.ShapeDtypeStruct(gate_up_weight.shape, BF16),
        ),
        in_specs=[anywhere] * 3,
        out_specs=(anywhere, anywhere),
        scratch_shapes=[
            pltpu.VMEM(fin.shape, BF16),
            pltpu.VMEM(slot_row.shape, jnp.int32),
            pltpu.VMEM(tokens.shape, BF16),
            pltpu.VMEM(gate_up_weight.shape, BF16),
            dma((4,)), dma((n_dp,)),
        ],
        compiler_params=pltpu.CompilerParams(vmem_limit_bytes=58 * 1024 * 1024),
        name="place_rows",
    )(fin, slot_row, grad_gate_up)


def solution(mesh):
    in_specs = (
        P(("dp", "expert"), None),
        P(("dp", "expert"), None),
        P(("dp", "expert"), None),
        P(("dp", "expert"), None),
        P("expert", "dp", None),
        P("expert", None, "dp"),
    )
    out_specs = (P(("dp", "expert"), None), P("expert", "dp", None))
    return jax.shard_map(
        functools.partial(on_device, mesh.shape["dp"]),
        mesh=mesh, in_specs=in_specs, out_specs=out_specs, check_vma=False,
    )
```

```python
import functools

import jax
import jax.numpy as jnp
from jax import lax
from jax.experimental import pallas as pl
from jax.experimental.pallas import tpu as pltpu
from jax.sharding import PartitionSpec as P

GROUP = 8
CAP = 8
MESH = pl.DeviceIdType.MESH
F32 = jnp.float32
BF16 = jnp.bfloat16
NT = (((1,), (1,)), ((), ()))
TN = (((0,), (0,)), ((), ()))


def kernel(
    n_dp, windows,
    tok_hbm, dy_hbm, slot_hbm, gate_hbm, gu_hbm, down_hbm,
    fin_ref, gw_hbm,
    tok_ref, dy_ref, slot_ref, gate_ref, gu_ref, down_ref, gw_ref,
    pick, buf, xall, part, prcv, dgrcv, dguall, dxs, across, sums, ret, gut, downt,
    s_in, s_out,
    s_pick, r_pick, s_ag, r_ag, s_rs, r_rs, s_dg, r_dg, s_cross, r_cross, s_ret, r_ret,
):
    S = GROUP
    Z = S // 2
    W = windows
    n_same = n_dp * W
    tokens, width = tok_ref.shape
    cols = width // n_dp
    half = cols // 2
    hidden = down_ref.shape[0]
    rows = n_dp * W * CAP
    me_d = lax.axis_index("dp")
    me_x = lax.axis_index("expert")
    me_w = me_x // S
    me_s = me_x % S
    zz = me_s // 2
    yy = me_s % 2

    def member(z, y):
        return (me_d, me_w * S + z * 2 + y)

    small = [
        pltpu.make_async_copy(slot_hbm, slot_ref, s_in.at[0]),
        pltpu.make_async_copy(gate_hbm, gate_ref, s_in.at[1]),
    ]
    big = []
    for d in range(n_dp):
        cut = pl.ds(d * cols, cols)
        at = 4 + 2 * d
        big.append(pltpu.make_async_copy(tok_hbm.at[:, cut], tok_ref.at[:, cut], s_in.at[at]))
        big.append(pltpu.make_async_copy(dy_hbm.at[:, cut], dy_ref.at[:, cut], s_in.at[at + 1]))
    down_in = pltpu.make_async_copy(down_hbm, down_ref, s_in.at[2])
    gu_in = pltpu.make_async_copy(gu_hbm, gu_ref, s_in.at[3])
    for copy in small + big + [down_in, gu_in]:
        copy.start()

    barrier = pltpu.get_barrier_semaphore()
    n_peer = n_same * Z
    me_flat = (me_d * W + me_w) * Z + zz

    def greet(k, carry):
        flat = (me_flat + k) % n_peer
        owner = flat // Z
        target = (owner // W, (owner % W) * S + (flat % Z) * 2 + yy)
        pl.semaphore_signal(barrier, inc=1, device_id=target, device_id_type=MESH)
        return carry

    lax.fori_loop(1, n_peer, greet, 0)
    pl.semaphore_signal(barrier, inc=1, device_id=member(zz, 1 - yy), device_id_type=MESH)

    def same(k):
        flat = (me_d * W + me_w + k) % n_same
        return flat // W, flat % W

    def pick_copy(h, d, w):
        return pltpu.make_async_remote_copy(
            src_ref=pick.at[h, d, w], dst_ref=buf.at[zz, yy, h, me_d, me_w],
            send_sem=s_pick.at[h, d, w], recv_sem=r_pick.at[h, me_d, me_w],
            device_id=(d, w * S + me_s), device_id_type=MESH,
        )

    def pick_arrival(h, d, w):
        return pltpu.make_async_remote_copy(
            src_ref=pick.at[h, d, w], dst_ref=buf.at[zz, yy, h, d, w],
            send_sem=s_pick.at[h, d, w], recv_sem=r_pick.at[h, d, w],
            device_id=(d, w * S + me_s), device_id_type=MESH,
        )

    for copy in small:
        copy.wait()
    place = lax.broadcasted_iota(jnp.int32, (CAP, tokens), 0)
    sels, weights = [], []
    for e in range(W):
        hit = slot_ref[e : e + 1, :] == place
        sels.append(jnp.where(hit, 1.0, 0.0).astype(BF16))
        weights.append(
            jnp.sum(jnp.where(hit, gate_ref[e : e + 1, :], 0.0), axis=1, keepdims=True)
        )
    for copy in big:
        copy.wait()
    for h in range(2):
        for e in range(W):
            for d in range(n_dp):
                cut = slice(d * cols + h * half, d * cols + (h + 1) * half)
                x = jnp.dot(sels[e], tok_ref[:, cut], preferred_element_type=F32)
                g = jnp.dot(sels[e], dy_ref[:, cut], preferred_element_type=F32) * weights[e]
                pick[h, d, e] = jnp.concatenate([x, g], axis=0).astype(BF16)
        if h == 0:
            pl.semaphore_wait(barrier, n_peer)
        for k in range(1, n_same):
            pick_copy(h, *same(k)).start()
        buf[zz, yy, h, me_d, me_w] = pick[h, me_d, me_w]
    down_in.wait()
    downt[...] = down_ref[...].T

    def spread(z, y, h, way, target):
        return pltpu.make_async_remote_copy(
            src_ref=buf.at[z, y, h], dst_ref=buf.at[z, y, h],
            send_sem=s_ag.at[z, h, way], recv_sem=r_ag.at[z, y, h],
            device_id=member(*target), device_id_type=MESH,
        )

    def reduce_copy(z, d, owner):
        return pltpu.make_async_remote_copy(
            src_ref=part.at[z, d], dst_ref=prcv.at[z, owner],
            send_sem=s_rs.at[z, d], recv_sem=r_rs.at[z, owner],
            device_id=(d, me_x), device_id_type=MESH,
        )

    def share_copy(z, d, owner):
        return pltpu.make_async_remote_copy(
            src_ref=dgrcv.at[z, me_d], dst_ref=dgrcv.at[z, owner],
            send_sem=s_dg.at[z, d], recv_sem=r_dg.at[z, owner],
            device_id=(d, me_x), device_id_type=MESH,
        )

    def cross_copy(z):
        return pltpu.make_async_remote_copy(
            src_ref=dxs.at[z, 1 - yy], dst_ref=across.at[z],
            send_sem=s_cross.at[z], recv_sem=r_cross.at[z],
            device_id=member(zz, 1 - yy), device_id_type=MESH,
        )

    def return_copy(z, d, w, owner_z, owner_d, owner_w):
        return pltpu.make_async_remote_copy(
            src_ref=sums.at[z, d, w], dst_ref=ret.at[owner_z, owner_d, owner_w],
            send_sem=s_ret.at[z, d, w], recv_sem=r_ret.at[owner_z, owner_d, owner_w],
            device_id=(d, w * S + z * 2 + yy), device_id_type=MESH,
        )

    def returns(z, act):
        for k in range(1, n_same):
            d, w = same(k)
            act(return_copy(z, d, w, zz, me_d, me_w))

        @pl.when(z != zz)
        def _():
            act(return_copy(z, me_d, me_w, zz, me_d, me_w))

    near = jnp.minimum(zz, Z - 1 - zz)

    def nth(m):
        alternating = ((m + 1) // 2) * (1 - 2 * (m % 2))
        far = m - near
        beyond = jnp.where(zz > Z - 1 - zz, -far, far)
        return zz + jnp.where(m <= 2 * near, alternating, beyond)

    def forward(z, h, act):
        @pl.when((z <= zz) & (zz + 1 < Z))
        def _():
            act(spread(z, yy, h, 0, (zz + 1, yy)))

        @pl.when((z >= zz) & (zz >= 1))
        def _():
            act(spread(z, yy, h, 1, (zz - 1, yy)))

        if h == 0:
            act(spread(z, yy, h, 2, (zz, 1 - yy)))
        else:

            @pl.when((z - zz != 1) & (zz - z != 1))
            def _():
                act(spread(z, yy, h, 2, (zz, 1 - yy)))

    def forward_other(act):
        @pl.when(zz + 1 < Z)
        def _():
            act(spread(zz, 1 - yy, 1, 3, (zz + 1, yy)))

        @pl.when(zz >= 1)
        def _():
            act(spread(zz, 1 - yy, 1, 4, (zz - 1, yy)))

    def start(copy):
        copy.start()

    def pass_on(k, h):
        @pl.when(zz - k >= 0)
        def _():
            spread(zz - k, yy, h, 2, (zz, 1 - yy)).wait_recv()
            forward(zz - k, h, start)

        @pl.when(zz + k < Z)
        def _():
            spread(zz + k, yy, h, 2, (zz, 1 - yy)).wait_recv()
            forward(zz + k, h, start)

    def arrive(m):
        z = nth(m)
        a_u = dh = 0.0
        for h in range(2):
            spread(z, 1 - yy, h, 2, (zz, 1 - yy)).wait_recv()
            if h == 1:

                @pl.when(m == 0)
                def _():
                    forward_other(start)

            both = buf[z, :, h].astype(F32).reshape(2 * n_dp * W, 2, CAP, half)
            x = both[:, 0].reshape(2 * rows, half).astype(BF16)
            g = both[:, 1].reshape(2 * rows, half).astype(BF16)
            cut = slice(h * half, (h + 1) * half)
            xall[z, :, cut] = x
            a_u = a_u + jnp.dot(x, gu_ref[cut], preferred_element_type=F32)
            dh = dh + jnp.dot(g, downt[cut], preferred_element_type=F32)
        a_u = a_u.reshape(2, n_dp, W * CAP, 2 * hidden)
        dh = dh.reshape(2, n_dp, W * CAP, hidden)
        part[z, :, :, : 2 * hidden] = jnp.concatenate([a_u[0], a_u[1]], axis=1).astype(BF16)
        part[z, :, :, 2 * hidden :] = jnp.concatenate([dh[0], dh[1]], axis=1).astype(BF16)
        for k in range(1, n_dp):
            reduce_copy(z, (me_d + k) % n_dp, me_d).start()

    def activate(m):
        z = nth(m)
        total = part[z, me_d].astype(F32)
        for k in range(1, n_dp):
            d = (me_d + k) % n_dp
            reduce_copy(z, d, d).wait_recv()
            total = total + prcv[z, d].astype(F32)
        pre = total[:, :hidden]
        up_part = total[:, hidden : 2 * hidden]
        dh = total[:, 2 * hidden :]
        sig = jax.nn.sigmoid(pre)
        dgate = dh * up_part * sig * (1.0 + pre * (1.0 - sig))
        dup = dh * (pre * sig)
        dgrcv[z, me_d] = jnp.concatenate(
            [dgate.reshape(2 * W, CAP, hidden), dup.reshape(2 * W, CAP, hidden)], axis=1
        ).astype(BF16)
        for k in range(1, n_dp):
            share_copy(z, (me_d + k) % n_dp, me_d).start()

    def give_back(m):
        z = nth(m)
        for k in range(1, n_dp):
            d = (me_d + k) % n_dp
            share_copy(z, d, d).wait_recv()
        both = dgrcv[z].astype(F32).reshape(n_dp, 2, W, 2, CAP, hidden)
        dgate = jnp.concatenate([both[:, y, :, 0].reshape(rows, hidden) for y in range(2)], axis=0)
        dup = jnp.concatenate([both[:, y, :, 1].reshape(rows, hidden) for y in range(2)], axis=0)
        dgu = jnp.concatenate([dgate, dup], axis=1).astype(BF16)
        dguall[z] = dgu
        dx = jnp.dot(dgu, gut[...], preferred_element_type=F32).astype(BF16)
        dxs[z] = dx.reshape(2, rows, cols)
        cross_copy(z).start()

    def combine(m):
        z = nth(m)
        cross_copy(z).wait_recv()
        both = dxs[z, yy].astype(F32) + across[z].astype(F32)
        both = both.reshape(n_dp, W, CAP, cols)
        sums[z] = jnp.concatenate([both[..., :half], both[..., half:]], axis=2).astype(BF16)
        returns(z, start)

    def step(m, carry):
        @pl.when(m < Z)
        def _():
            pass_on(m + 1, 1)
            arrive(m)
            pass_on(m + 2, 0)

        @pl.when((m >= 1) & (m < Z + 1))
        def _():
            activate(m - 1)

        @pl.when(m >= 2)
        def _():
            give_back(m - 2)

        @pl.when(m >= 3)
        def _():
            combine(m - 3)

        return carry

    for h in range(2):
        for k in range(1, n_same):
            pick_arrival(h, *same(k)).wait_recv()
        forward(zz, h, start)
    gu_in.wait()
    gut[...] = gu_ref[...].T
    pass_on(1, 0)
    lax.fori_loop(0, Z + 2, step, 0)

    def weight_gradient(h):
        cut = slice(h * half, (h + 1) * half)
        gw_ref[0, cut] = lax.dot_general(
            xall[:, :, cut].reshape(S * rows, half), dguall[...].reshape(S * rows, 2 * hidden), TN,
            preferred_element_type=F32,
        ).astype(BF16)

    def gradient_out(h):
        cut = pl.ds(h * half, half)
        return pltpu.make_async_copy(gw_ref.at[0, cut], gw_hbm.at[0, cut], s_out.at[h])

    weight_gradient(0)
    gradient_out(0).start()
    combine(Z - 1)
    weight_gradient(1)
    gradient_out(1).start()

    for k in range(1, n_same):
        for h in range(2):
            pick_copy(h, *same(k)).wait_send()

    def wait_send(copy):
        copy.wait_send()

    def drain(z, carry):
        for h in range(2):
            forward(z, h, wait_send)
        cross_copy(z).wait_send()
        for k in range(1, n_dp):
            d = (me_d + k) % n_dp
            reduce_copy(z, d, me_d).wait_send()
            share_copy(z, d, me_d).wait_send()
        returns(z, wait_send)
        return carry

    forward_other(wait_send)
    lax.fori_loop(0, Z, drain, 0)

    total = 0.0
    ret[zz, me_d, me_w] = sums[zz, me_d, me_w]
    for j in range(Z):
        z = (zz + j) % Z
        for k in range(1 if j == 0 else 0, n_same):
            d, w = same(k)
            return_copy(z, d, w, z, d, w).wait_recv()
        total = total + ret[z].astype(F32)
    fin_ref[...] = total.astype(BF16)
    gradient_out(0).wait()
    gradient_out(1).wait()


def place_rows(
    fin_hbm, slot_hbm, gw_in, gx_hbm, gw_hbm, fin_ref, slot_ref, gx_ref, s_in, s_out
):
    n_dp, W, _, half = fin_ref.shape
    tokens = gx_ref.shape[0]
    slot_copy = pltpu.make_async_copy(slot_hbm, slot_ref, s_in.at[0])
    fin_copy = pltpu.make_async_copy(fin_hbm, fin_ref, s_in.at[1])
    gw_copy = pltpu.make_async_copy(gw_in, gw_hbm, s_in.at[2])
    for copy in (slot_copy, fin_copy, gw_copy):
        copy.start()
    outs = []
    slot_copy.wait()
    place = lax.broadcasted_iota(jnp.int32, (2 * CAP, tokens), 0)
    hits = []
    for h in range(2):
        for e in range(W):
            hit = (slot_ref[e : e + 1, :] == place - h * CAP) & (place >= h * CAP)
            hits.append(jnp.where(hit, 1.0, 0.0).T.astype(BF16))
    fin_copy.wait()
    for d in range(n_dp):
        for h in range(2):
            out = jnp.dot(hits[h * W], fin_ref[d, 0], preferred_element_type=F32)
            for e in range(1, W):
                out = out + jnp.dot(hits[h * W + e], fin_ref[d, e], preferred_element_type=F32)
            at = (2 * d + h) * half
            gx_ref[:, at : at + half] = out.astype(BF16)
        cut = pl.ds(2 * d * half, 2 * half)
        outs.append(pltpu.make_async_copy(gx_ref.at[:, cut], gx_hbm.at[:, cut], s_out.at[d]))
        outs[d].start()
    for copy in outs:
        copy.wait()
    gw_copy.wait()


def on_device(n_dp, tokens, output_gradient, slot, gate_weight, gate_up_weight, down_weight):
    W = slot.shape[1]
    S = GROUP
    Z = S // 2
    _, cols, wide = gate_up_weight.shape
    hidden = wide // 2
    rows = n_dp * W * CAP
    vmem = pl.BlockSpec(memory_space=pltpu.VMEM)
    anywhere = pl.BlockSpec(memory_space=pl.ANY)
    dma = pltpu.SemaphoreType.DMA
    slot_row = slot.T
    fin, grad_gate_up = pl.pallas_call(
        functools.partial(kernel, n_dp, W),
        out_shape=(
            jax.ShapeDtypeStruct((n_dp, W, 2 * CAP, cols // 2), BF16),
            jax.ShapeDtypeStruct(gate_up_weight.shape, BF16),
        ),
        in_specs=[anywhere] * 6,
        out_specs=(vmem, anywhere),
        scratch_shapes=[
            pltpu.VMEM(tokens.shape, BF16),
            pltpu.VMEM(tokens.shape, BF16),
            pltpu.VMEM(slot_row.shape, jnp.int32),
            pltpu.VMEM(slot_row.shape, F32),
            pltpu.VMEM((cols, wide), BF16),
            pltpu.VMEM((hidden, cols), BF16),
            pltpu.VMEM((1, cols, wide), BF16),
            pltpu.VMEM((2, n_dp, W, 2 * CAP, cols // 2), BF16),
            pltpu.VMEM((Z, 2, 2, n_dp, W, 2 * CAP, cols // 2), BF16),
            pltpu.VMEM((Z, 2 * rows, cols), BF16),
            pltpu.VMEM((Z, n_dp, 2 * W * CAP, 3 * hidden), BF16),
            pltpu.VMEM((Z, n_dp, 2 * W * CAP, 3 * hidden), BF16),
            pltpu.VMEM((Z, n_dp, 2 * W, 2 * CAP, hidden), BF16),
            pltpu.VMEM((Z, 2 * rows, wide), BF16),
            pltpu.VMEM((Z, 2, rows, cols), BF16),
            pltpu.VMEM((Z, rows, cols), BF16),
            pltpu.VMEM((Z, n_dp, W, 2 * CAP, cols // 2), BF16),
            pltpu.VMEM((Z, n_dp, W, 2 * CAP, cols // 2), BF16),
            pltpu.VMEM((wide, cols), BF16),
            pltpu.VMEM((cols, hidden), BF16),
            dma((4 + 2 * n_dp,)), dma((2,)),
            dma((2, n_dp, W)), dma((2, n_dp, W)),
            dma((Z, 2, 5)), dma((Z, 2, 2)),
            dma((Z, n_dp)), dma((Z, n_dp)),
            dma((Z, n_dp)), dma((Z, n_dp)),
            dma((Z,)), dma((Z,)),
            dma((Z, n_dp, W)), dma((Z, n_dp, W)),
        ],
        compiler_params=pltpu.CompilerParams(
            collective_id=0, has_side_effects=True, vmem_limit_bytes=58 * 1024 * 1024
        ),
        cost_estimate=pl.CostEstimate(
            flops=14 * S * rows * cols * hidden,
            bytes_accessed=4 * tokens.size + 4 * gate_up_weight.size, transcendentals=0,
        ),
        name="routed_backward",
    )(tokens, output_gradient, slot_row, gate_weight.T, gate_up_weight[0], down_weight[0])
    return pl.pallas_call(
        place_rows,
        out_shape=(
            jax.ShapeDtypeStruct(tokens.shape, BF16),
            jax.ShapeDtypeStruct(gate_up_weight.shape, BF16),
        ),
        in_specs=[anywhere] * 3,
        out_specs=(anywhere, anywhere),
        scratch_shapes=[
            pltpu.VMEM(fin.shape, BF16),
            pltpu.VMEM(slot_row.shape, jnp.int32),
            pltpu.VMEM(tokens.shape, BF16),
            dma((3,)), dma((n_dp,)),
        ],
        compiler_params=pltpu.CompilerParams(vmem_limit_bytes=58 * 1024 * 1024),
        name="place_rows",
    )(fin, slot_row, grad_gate_up)


def solution(mesh):
    in_specs = (
        P(("dp", "expert"), None),
        P(("dp", "expert"), None),
        P(("dp", "expert"), None),
        P(("dp", "expert"), None),
        P("expert", "dp", None),
        P("expert", None, "dp"),
    )
    out_specs = (P(("dp", "expert"), None), P("expert", "dp", None))
    return jax.shard_map(
        functools.partial(on_device, mesh.shape["dp"]),
        mesh=mesh, in_specs=in_specs, out_specs=out_specs, check_vma=False,
    )
```

```python
import functools

import jax
import jax.numpy as jnp
from jax import lax
from jax.experimental import pallas as pl
from jax.experimental.pallas import tpu as pltpu
from jax.sharding import PartitionSpec as P

GROUP = 8
CAP = 8
MESH = pl.DeviceIdType.MESH
F32 = jnp.float32
BF16 = jnp.bfloat16
NT = (((1,), (1,)), ((), ()))
TN = (((0,), (0,)), ((), ()))


def kernel(
    n_dp, windows,
    tok_hbm, dy_hbm, slot_hbm, gate_hbm, gu_hbm, down_hbm,
    fin_ref, gw_hbm,
    tok_ref, dy_ref, slot_ref, gate_ref, gu_ref, down_ref, gw_ref,
    pick, buf, xall, part, prcv, dgrcv, dguall, dxs, across, sums, ret, gut, downt,
    s_in, s_out,
    s_pick, r_pick, s_ag, r_ag, s_rs, r_rs, s_dg, r_dg, s_cross, r_cross, s_ret, r_ret,
):
    S = GROUP
    Z = S // 2
    W = windows
    n_same = n_dp * W
    tokens, width = tok_ref.shape
    cols = width // n_dp
    half = cols // 2
    hidden = down_ref.shape[0]
    rows = n_dp * W * CAP
    me_d = lax.axis_index("dp")
    me_x = lax.axis_index("expert")
    me_w = me_x // S
    me_s = me_x % S
    zz = me_s // 2
    yy = me_s % 2

    def member(z, y):
        return (me_d, me_w * S + z * 2 + y)

    small = [
        pltpu.make_async_copy(slot_hbm, slot_ref, s_in.at[0]),
        pltpu.make_async_copy(gate_hbm, gate_ref, s_in.at[1]),
    ]
    big = []
    for d in range(n_dp):
        cut = pl.ds(d * cols, cols)
        at = 4 + 2 * d
        big.append(pltpu.make_async_copy(tok_hbm.at[:, cut], tok_ref.at[:, cut], s_in.at[at]))
        big.append(pltpu.make_async_copy(dy_hbm.at[:, cut], dy_ref.at[:, cut], s_in.at[at + 1]))
    down_in = pltpu.make_async_copy(down_hbm, down_ref, s_in.at[2])
    gu_in = pltpu.make_async_copy(gu_hbm, gu_ref, s_in.at[3])
    for copy in small + big + [down_in, gu_in]:
        copy.start()

    barrier = pltpu.get_barrier_semaphore()
    n_peer = n_same * Z
    me_flat = (me_d * W + me_w) * Z + zz

    def greet(k, carry):
        flat = (me_flat + k) % n_peer
        owner = flat // Z
        target = (owner // W, (owner % W) * S + (flat % Z) * 2 + yy)
        pl.semaphore_signal(barrier, inc=1, device_id=target, device_id_type=MESH)
        return carry

    lax.fori_loop(1, n_peer, greet, 0)
    pl.semaphore_signal(barrier, inc=1, device_id=member(zz, 1 - yy), device_id_type=MESH)

    def same(k):
        flat = (me_d * W + me_w + k) % n_same
        return flat // W, flat % W

    def pick_copy(h, d, w):
        return pltpu.make_async_remote_copy(
            src_ref=pick.at[h, d, w], dst_ref=buf.at[zz, yy, h, me_d, me_w],
            send_sem=s_pick.at[h, d, w], recv_sem=r_pick.at[h, me_d, me_w],
            device_id=(d, w * S + me_s), device_id_type=MESH,
        )

    def pick_arrival(h, d, w):
        return pltpu.make_async_remote_copy(
            src_ref=pick.at[h, d, w], dst_ref=buf.at[zz, yy, h, d, w],
            send_sem=s_pick.at[h, d, w], recv_sem=r_pick.at[h, d, w],
            device_id=(d, w * S + me_s), device_id_type=MESH,
        )

    for copy in small:
        copy.wait()
    place = lax.broadcasted_iota(jnp.int32, (CAP, tokens), 0)
    sels, weights = [], []
    for e in range(W):
        hit = slot_ref[e : e + 1, :] == place
        sels.append(jnp.where(hit, 1.0, 0.0).astype(BF16))
        weights.append(
            jnp.sum(jnp.where(hit, gate_ref[e : e + 1, :], 0.0), axis=1, keepdims=True)
        )
    for copy in big:
        copy.wait()
    for h in range(2):
        for e in range(W):
            for d in range(n_dp):
                cut = slice(d * cols + h * half, d * cols + (h + 1) * half)
                x = jnp.dot(sels[e], tok_ref[:, cut], preferred_element_type=F32)
                g = jnp.dot(sels[e], dy_ref[:, cut], preferred_element_type=F32) * weights[e]
                pick[h, d, e] = jnp.concatenate([x, g], axis=0).astype(BF16)
        if h == 0:
            pl.semaphore_wait(barrier, n_peer)
        for k in range(1, n_same):
            pick_copy(h, *same(k)).start()
        buf[zz, yy, h, me_d, me_w] = pick[h, me_d, me_w]
    down_in.wait()
    downt[...] = down_ref[...].T

    def spread(z, y, h, way, target):
        return pltpu.make_async_remote_copy(
            src_ref=buf.at[z, y, h], dst_ref=buf.at[z, y, h],
            send_sem=s_ag.at[z, h, way], recv_sem=r_ag.at[z, y, h],
            device_id=member(*target), device_id_type=MESH,
        )

    def reduce_copy(z, d, owner):
        return pltpu.make_async_remote_copy(
            src_ref=part.at[z, d], dst_ref=prcv.at[z, owner],
            send_sem=s_rs.at[z, d], recv_sem=r_rs.at[z, owner],
            device_id=(d, me_x), device_id_type=MESH,
        )

    def share_copy(z, d, owner):
        return pltpu.make_async_remote_copy(
            src_ref=dgrcv.at[z, me_d], dst_ref=dgrcv.at[z, owner],
            send_sem=s_dg.at[z, d], recv_sem=r_dg.at[z, owner],
            device_id=(d, me_x), device_id_type=MESH,
        )

    def cross_copy(z):
        return pltpu.make_async_remote_copy(
            src_ref=dxs.at[z, 1 - yy], dst_ref=across.at[z],
            send_sem=s_cross.at[z], recv_sem=r_cross.at[z],
            device_id=member(zz, 1 - yy), device_id_type=MESH,
        )

    def return_copy(z, d, w, owner_z, owner_d, owner_w):
        return pltpu.make_async_remote_copy(
            src_ref=sums.at[z, d, w], dst_ref=ret.at[owner_z, owner_d, owner_w],
            send_sem=s_ret.at[z, d, w], recv_sem=r_ret.at[owner_z, owner_d, owner_w],
            device_id=(d, w * S + z * 2 + yy), device_id_type=MESH,
        )

    def returns(z, act):
        for k in range(1, n_same):
            d, w = same(k)
            act(return_copy(z, d, w, zz, me_d, me_w))

        @pl.when(z != zz)
        def _():
            act(return_copy(z, me_d, me_w, zz, me_d, me_w))

    near = jnp.minimum(zz, Z - 1 - zz)

    def nth(m):
        alternating = ((m + 1) // 2) * (1 - 2 * (m % 2))
        far = m - near
        beyond = jnp.where(zz > Z - 1 - zz, -far, far)
        return zz + jnp.where(m <= 2 * near, alternating, beyond)

    def forward(z, h, act):
        @pl.when((z <= zz) & (zz + 1 < Z) & (zz - z < Z - 2))
        def _():
            act(spread(z, yy, h, 0, (zz + 1, yy)))

        @pl.when((z >= zz) & (zz >= 1) & (z - zz < Z - 2))
        def _():
            act(spread(z, yy, h, 1, (zz - 1, yy)))

        if h == 0:
            act(spread(z, yy, h, 2, (zz, 1 - yy)))
        else:

            @pl.when((z - zz != 1) & (zz - z != 1))
            def _():
                act(spread(z, yy, h, 2, (zz, 1 - yy)))

    def forward_other(act):
        @pl.when(zz + 1 < Z)
        def _():
            act(spread(zz, 1 - yy, 1, 3, (zz + 1, yy)))

        @pl.when(zz >= 1)
        def _():
            act(spread(zz, 1 - yy, 1, 4, (zz - 1, yy)))

    def forward_far(h, act):
        @pl.when(zz == 0)
        def _():
            act(spread(zz, yy, h, 5, (Z - 1, yy)))

        @pl.when(zz == Z - 1)
        def _():
            act(spread(zz, yy, h, 5, (0, yy)))

    def start(copy):
        copy.start()

    def pass_on(k, h):
        @pl.when(zz - k >= 0)
        def _():
            spread(zz - k, yy, h, 2, (zz, 1 - yy)).wait_recv()
            forward(zz - k, h, start)

        @pl.when(zz + k < Z)
        def _():
            spread(zz + k, yy, h, 2, (zz, 1 - yy)).wait_recv()
            forward(zz + k, h, start)

    def arrive(m):
        z = nth(m)
        a_u = dh = 0.0
        for h in range(2):
            spread(z, 1 - yy, h, 2, (zz, 1 - yy)).wait_recv()
            if h == 1:

                @pl.when(m == 0)
                def _():
                    forward_other(start)

            both = buf[z, :, h].astype(F32).reshape(2 * n_dp * W, 2, CAP, half)
            x = both[:, 0].reshape(2 * rows, half).astype(BF16)
            g = both[:, 1].reshape(2 * rows, half).astype(BF16)
            cut = slice(h * half, (h + 1) * half)
            xall[z, :, cut] = x
            a_u = a_u + jnp.dot(x, gu_ref[cut], preferred_element_type=F32)
            dh = dh + jnp.dot(g, downt[cut], preferred_element_type=F32)
        a_u = a_u.reshape(2, n_dp, W * CAP, 2 * hidden)
        dh = dh.reshape(2, n_dp, W * CAP, hidden)
        part[z, :, :, : 2 * hidden] = jnp.concatenate([a_u[0], a_u[1]], axis=1).astype(BF16)
        part[z, :, :, 2 * hidden :] = jnp.concatenate([dh[0], dh[1]], axis=1).astype(BF16)
        for k in range(1, n_dp):
            reduce_copy(z, (me_d + k) % n_dp, me_d).start()

    def activate(m):
        z = nth(m)
        total = part[z, me_d].astype(F32)
        for k in range(1, n_dp):
            d = (me_d + k) % n_dp
            reduce_copy(z, d, d).wait_recv()
            total = total + prcv[z, d].astype(F32)
        pre = total[:, :hidden]
        up_part = total[:, hidden : 2 * hidden]
        dh = total[:, 2 * hidden :]
        sig = jax.nn.sigmoid(pre)
        dgate = dh * up_part * sig * (1.0 + pre * (1.0 - sig))
        dup = dh * (pre * sig)
        dgrcv[z, me_d] = jnp.concatenate(
            [dgate.reshape(2 * W, CAP, hidden), dup.reshape(2 * W, CAP, hidden)], axis=1
        ).astype(BF16)
        for k in range(1, n_dp):
            share_copy(z, (me_d + k) % n_dp, me_d).start()

    def give_back(m):
        z = nth(m)
        for k in range(1, n_dp):
            d = (me_d + k) % n_dp
            share_copy(z, d, d).wait_recv()
        both = dgrcv[z].astype(F32).reshape(n_dp, 2, W, 2, CAP, hidden)
        dgate = jnp.concatenate([both[:, y, :, 0].reshape(rows, hidden) for y in range(2)], axis=0)
        dup = jnp.concatenate([both[:, y, :, 1].reshape(rows, hidden) for y in range(2)], axis=0)
        dgu = jnp.concatenate([dgate, dup], axis=1).astype(BF16)
        dguall[z] = dgu
        dx = jnp.dot(dgu, gut[...], preferred_element_type=F32).astype(BF16)
        dxs[z] = dx.reshape(2, rows, cols)
        cross_copy(z).start()

    def combine(m):
        z = nth(m)
        cross_copy(z).wait_recv()
        both = dxs[z, yy].astype(F32) + across[z].astype(F32)
        both = both.reshape(n_dp, W, CAP, cols)
        sums[z] = jnp.concatenate([both[..., :half], both[..., half:]], axis=2).astype(BF16)
        returns(z, start)

    def step(m, carry):
        @pl.when(m < Z)
        def _():
            pass_on(m + 1, 1)
            arrive(m)
            pass_on(m + 2, 0)

        @pl.when((m >= 1) & (m < Z + 1))
        def _():
            activate(m - 1)

        @pl.when(m >= 2)
        def _():
            give_back(m - 2)

        @pl.when(m >= 3)
        def _():
            combine(m - 3)

        return carry

    for h in range(2):
        for k in range(1, n_same):
            pick_arrival(h, *same(k)).wait_recv()
        forward(zz, h, start)
    for h in range(2):
        forward_far(h, start)
    gu_in.wait()
    gut[...] = gu_ref[...].T
    pass_on(1, 0)
    lax.fori_loop(0, Z + 2, step, 0)

    def weight_gradient(h):
        cut = slice(h * half, (h + 1) * half)
        gw_ref[0, cut] = lax.dot_general(
            xall[:, :, cut].reshape(S * rows, half), dguall[...].reshape(S * rows, 2 * hidden), TN,
            preferred_element_type=F32,
        ).astype(BF16)

    def gradient_out(h):
        cut = pl.ds(h * half, half)
        return pltpu.make_async_copy(gw_ref.at[0, cut], gw_hbm.at[0, cut], s_out.at[h])

    weight_gradient(0)
    gradient_out(0).start()
    combine(Z - 1)
    weight_gradient(1)
    gradient_out(1).start()

    for k in range(1, n_same):
        for h in range(2):
            pick_copy(h, *same(k)).wait_send()

    def wait_send(copy):
        copy.wait_send()

    def drain(z, carry):
        for h in range(2):
            forward(z, h, wait_send)
        cross_copy(z).wait_send()
        for k in range(1, n_dp):
            d = (me_d + k) % n_dp
            reduce_copy(z, d, me_d).wait_send()
            share_copy(z, d, me_d).wait_send()
        returns(z, wait_send)
        return carry

    forward_other(wait_send)
    for h in range(2):
        forward_far(h, wait_send)
    lax.fori_loop(0, Z, drain, 0)

    total = 0.0
    ret[zz, me_d, me_w] = sums[zz, me_d, me_w]
    for j in range(Z):
        z = (zz + j) % Z
        for k in range(1 if j == 0 else 0, n_same):
            d, w = same(k)
            return_copy(z, d, w, z, d, w).wait_recv()
        total = total + ret[z].astype(F32)
    fin_ref[...] = total.astype(BF16)
    gradient_out(0).wait()
    gradient_out(1).wait()


def place_rows(
    fin_hbm, slot_hbm, gw_in, gx_hbm, gw_hbm, fin_ref, slot_ref, gx_ref, gw_ref, s_in, s_out
):
    n_dp, W, _, half = fin_ref.shape
    tokens = gx_ref.shape[0]
    slot_copy = pltpu.make_async_copy(slot_hbm, slot_ref, s_in.at[0])
    fin_copy = pltpu.make_async_copy(fin_hbm, fin_ref, s_in.at[1])
    gw_copy = pltpu.make_async_copy(gw_in, gw_ref, s_in.at[2])
    for copy in (slot_copy, fin_copy, gw_copy):
        copy.start()
    gw_out = pltpu.make_async_copy(gw_ref, gw_hbm, s_in.at[3])
    outs = []
    slot_copy.wait()
    place = lax.broadcasted_iota(jnp.int32, (2 * CAP, tokens), 0)
    hits = []
    for h in range(2):
        for e in range(W):
            hit = (slot_ref[e : e + 1, :] == place - h * CAP) & (place >= h * CAP)
            hits.append(jnp.where(hit, 1.0, 0.0).T.astype(BF16))
    gw_copy.wait()
    gw_out.start()
    fin_copy.wait()
    for d in range(n_dp):
        for h in range(2):
            out = jnp.dot(hits[h * W], fin_ref[d, 0], preferred_element_type=F32)
            for e in range(1, W):
                out = out + jnp.dot(hits[h * W + e], fin_ref[d, e], preferred_element_type=F32)
            at = (2 * d + h) * half
            gx_ref[:, at : at + half] = out.astype(BF16)
        cut = pl.ds(2 * d * half, 2 * half)
        outs.append(pltpu.make_async_copy(gx_ref.at[:, cut], gx_hbm.at[:, cut], s_out.at[d]))
        outs[d].start()
    for copy in outs:
        copy.wait()
    gw_out.wait()


def on_device(n_dp, tokens, output_gradient, slot, gate_weight, gate_up_weight, down_weight):
    W = slot.shape[1]
    S = GROUP
    Z = S // 2
    _, cols, wide = gate_up_weight.shape
    hidden = wide // 2
    rows = n_dp * W * CAP
    vmem = pl.BlockSpec(memory_space=pltpu.VMEM)
    anywhere = pl.BlockSpec(memory_space=pl.ANY)
    dma = pltpu.SemaphoreType.DMA
    slot_row = slot.T
    fin, grad_gate_up = pl.pallas_call(
        functools.partial(kernel, n_dp, W),
        out_shape=(
            jax.ShapeDtypeStruct((n_dp, W, 2 * CAP, cols // 2), BF16),
            jax.ShapeDtypeStruct(gate_up_weight.shape, BF16),
        ),
        in_specs=[anywhere] * 6,
        out_specs=(vmem, anywhere),
        scratch_shapes=[
            pltpu.VMEM(tokens.shape, BF16),
            pltpu.VMEM(tokens.shape, BF16),
            pltpu.VMEM(slot_row.shape, jnp.int32),
            pltpu.VMEM(slot_row.shape, F32),
            pltpu.VMEM((cols, wide), BF16),
            pltpu.VMEM((hidden, cols), BF16),
            pltpu.VMEM((1, cols, wide), BF16),
            pltpu.VMEM((2, n_dp, W, 2 * CAP, cols // 2), BF16),
            pltpu.VMEM((Z, 2, 2, n_dp, W, 2 * CAP, cols // 2), BF16),
            pltpu.VMEM((Z, 2 * rows, cols), BF16),
            pltpu.VMEM((Z, n_dp, 2 * W * CAP, 3 * hidden), BF16),
            pltpu.VMEM((Z, n_dp, 2 * W * CAP, 3 * hidden), BF16),
            pltpu.VMEM((Z, n_dp, 2 * W, 2 * CAP, hidden), BF16),
            pltpu.VMEM((Z, 2 * rows, wide), BF16),
            pltpu.VMEM((Z, 2, rows, cols), BF16),
            pltpu.VMEM((Z, rows, cols), BF16),
            pltpu.VMEM((Z, n_dp, W, 2 * CAP, cols // 2), BF16),
            pltpu.VMEM((Z, n_dp, W, 2 * CAP, cols // 2), BF16),
            pltpu.VMEM((wide, cols), BF16),
            pltpu.VMEM((cols, hidden), BF16),
            dma((4 + 2 * n_dp,)), dma((2,)),
            dma((2, n_dp, W)), dma((2, n_dp, W)),
            dma((Z, 2, 6)), dma((Z, 2, 2)),
            dma((Z, n_dp)), dma((Z, n_dp)),
            dma((Z, n_dp)), dma((Z, n_dp)),
            dma((Z,)), dma((Z,)),
            dma((Z, n_dp, W)), dma((Z, n_dp, W)),
        ],
        compiler_params=pltpu.CompilerParams(
            collective_id=0, has_side_effects=True, vmem_limit_bytes=58 * 1024 * 1024
        ),
        cost_estimate=pl.CostEstimate(
            flops=14 * S * rows * cols * hidden,
            bytes_accessed=4 * tokens.size + 4 * gate_up_weight.size, transcendentals=0,
        ),
        name="routed_backward",
    )(tokens, output_gradient, slot_row, gate_weight.T, gate_up_weight[0], down_weight[0])
    return pl.pallas_call(
        place_rows,
        out_shape=(
            jax.ShapeDtypeStruct(tokens.shape, BF16),
            jax.ShapeDtypeStruct(gate_up_weight.shape, BF16),
        ),
        in_specs=[anywhere] * 3,
        out_specs=(anywhere, anywhere),
        scratch_shapes=[
            pltpu.VMEM(fin.shape, BF16),
            pltpu.VMEM(slot_row.shape, jnp.int32),
            pltpu.VMEM(tokens.shape, BF16),
            pltpu.VMEM(gate_up_weight.shape, BF16),
            dma((4,)), dma((n_dp,)),
        ],
        compiler_params=pltpu.CompilerParams(vmem_limit_bytes=58 * 1024 * 1024),
        name="place_rows",
    )(fin, slot_row, grad_gate_up)


def solution(mesh):
    in_specs = (
        P(("dp", "expert"), None),
        P(("dp", "expert"), None),
        P(("dp", "expert"), None),
        P(("dp", "expert"), None),
        P("expert", "dp", None),
        P("expert", None, "dp"),
    )
    out_specs = (P(("dp", "expert"), None), P("expert", "dp", None))
    return jax.shard_map(
        functools.partial(on_device, mesh.shape["dp"]),
        mesh=mesh, in_specs=in_specs, out_specs=out_specs, check_vma=False,
    )
```

```python
import functools

import jax
import jax.numpy as jnp
from jax import lax
from jax.experimental import pallas as pl
from jax.experimental.pallas import tpu as pltpu
from jax.sharding import PartitionSpec as P

GROUP = 8
CAP = 8
MESH = pl.DeviceIdType.MESH
F32 = jnp.float32
BF16 = jnp.bfloat16
NT = (((1,), (1,)), ((), ()))
TN = (((0,), (0,)), ((), ()))


def kernel(
    n_dp, windows,
    tok_hbm, dy_hbm, slot_hbm, gate_hbm, gu_hbm, down_hbm,
    fin_ref, gw_hbm,
    tok_ref, dy_ref, slot_ref, gate_ref, gu_ref, down_ref, gw_ref,
    pick, buf, xall, part, prcv, dgrcv, dguall, dxs, across, sums, ret, gut, downt,
    s_in, s_out,
    s_pick, r_pick, s_ag, r_ag, s_rs, r_rs, s_dg, r_dg, s_cross, r_cross, s_ret, r_ret,
):
    S = GROUP
    Z = S // 2
    W = windows
    n_same = n_dp * W
    tokens, width = tok_ref.shape
    cols = width // n_dp
    half = cols // 2
    hidden = down_ref.shape[0]
    rows = n_dp * W * CAP
    me_d = lax.axis_index("dp")
    me_x = lax.axis_index("expert")
    me_w = me_x // S
    me_s = me_x % S
    zz = me_s // 2
    yy = me_s % 2

    def member(z, y):
        return (me_d, me_w * S + z * 2 + y)

    small = [
        pltpu.make_async_copy(slot_hbm, slot_ref, s_in.at[0]),
        pltpu.make_async_copy(gate_hbm, gate_ref, s_in.at[1]),
    ]
    big = []
    for d in range(n_dp):
        cut = pl.ds(d * cols, cols)
        at = 4 + 2 * d
        big.append(pltpu.make_async_copy(tok_hbm.at[:, cut], tok_ref.at[:, cut], s_in.at[at]))
        big.append(pltpu.make_async_copy(dy_hbm.at[:, cut], dy_ref.at[:, cut], s_in.at[at + 1]))
    down_in = pltpu.make_async_copy(down_hbm, down_ref, s_in.at[2])
    gu_in = pltpu.make_async_copy(gu_hbm, gu_ref, s_in.at[3])
    for copy in small + big + [down_in, gu_in]:
        copy.start()

    barrier = pltpu.get_barrier_semaphore()
    n_peer = n_same * Z
    me_flat = (me_d * W + me_w) * Z + zz

    def greet(k, carry):
        flat = (me_flat + k) % n_peer
        owner = flat // Z
        target = (owner // W, (owner % W) * S + (flat % Z) * 2 + yy)
        pl.semaphore_signal(barrier, inc=1, device_id=target, device_id_type=MESH)
        return carry

    lax.fori_loop(1, n_peer, greet, 0)
    pl.semaphore_signal(barrier, inc=1, device_id=member(zz, 1 - yy), device_id_type=MESH)

    def same(k):
        flat = (me_d * W + me_w + k) % n_same
        return flat // W, flat % W

    def pick_copy(h, d, w):
        return pltpu.make_async_remote_copy(
            src_ref=pick.at[h, d, w], dst_ref=buf.at[zz, yy, h, me_d, me_w],
            send_sem=s_pick.at[h, d, w], recv_sem=r_pick.at[h, me_d, me_w],
            device_id=(d, w * S + me_s), device_id_type=MESH,
        )

    def pick_arrival(h, d, w):
        return pltpu.make_async_remote_copy(
            src_ref=pick.at[h, d, w], dst_ref=buf.at[zz, yy, h, d, w],
            send_sem=s_pick.at[h, d, w], recv_sem=r_pick.at[h, d, w],
            device_id=(d, w * S + me_s), device_id_type=MESH,
        )

    for copy in small:
        copy.wait()
    place = lax.broadcasted_iota(jnp.int32, (CAP, tokens), 0)
    sels, weights = [], []
    for e in range(W):
        hit = slot_ref[e : e + 1, :] == place
        sels.append(jnp.where(hit, 1.0, 0.0).astype(BF16))
        weights.append(
            jnp.sum(jnp.where(hit, gate_ref[e : e + 1, :], 0.0), axis=1, keepdims=True)
        )
    for d in range(n_dp):
        big[2 * d].wait()
        big[2 * d + 1].wait()
        for h in range(2):
            cut = slice(d * cols + h * half, d * cols + (h + 1) * half)
            for e in range(W):
                x = jnp.dot(sels[e], tok_ref[:, cut], preferred_element_type=F32)
                g = jnp.dot(sels[e], dy_ref[:, cut], preferred_element_type=F32) * weights[e]
                pick[h, d, e] = jnp.concatenate([x, g], axis=0).astype(BF16)
            if d == 0 and h == 0:
                pl.semaphore_wait(barrier, n_peer)
            for e in range(W):

                @pl.when((me_d != d) | (me_w != e))
                def _():
                    pick_copy(h, d, e).start()

    for h in range(2):
        buf[zz, yy, h, me_d, me_w] = pick[h, me_d, me_w]
    down_in.wait()
    downt[...] = down_ref[...].T

    def spread(z, y, h, way, target):
        return pltpu.make_async_remote_copy(
            src_ref=buf.at[z, y, h], dst_ref=buf.at[z, y, h],
            send_sem=s_ag.at[z, h, way], recv_sem=r_ag.at[z, y, h],
            device_id=member(*target), device_id_type=MESH,
        )

    def reduce_copy(z, d, owner):
        return pltpu.make_async_remote_copy(
            src_ref=part.at[z, d], dst_ref=prcv.at[z, owner],
            send_sem=s_rs.at[z, d], recv_sem=r_rs.at[z, owner],
            device_id=(d, me_x), device_id_type=MESH,
        )

    def share_copy(z, d, owner):
        return pltpu.make_async_remote_copy(
            src_ref=dgrcv.at[z, me_d], dst_ref=dgrcv.at[z, owner],
            send_sem=s_dg.at[z, d], recv_sem=r_dg.at[z, owner],
            device_id=(d, me_x), device_id_type=MESH,
        )

    def cross_copy(z):
        return pltpu.make_async_remote_copy(
            src_ref=dxs.at[z, 1 - yy], dst_ref=across.at[z],
            send_sem=s_cross.at[z], recv_sem=r_cross.at[z],
            device_id=member(zz, 1 - yy), device_id_type=MESH,
        )

    def return_copy(z, d, w, owner_z, owner_d, owner_w):
        return pltpu.make_async_remote_copy(
            src_ref=sums.at[z, d, w], dst_ref=ret.at[owner_z, owner_d, owner_w],
            send_sem=s_ret.at[z, d, w], recv_sem=r_ret.at[owner_z, owner_d, owner_w],
            device_id=(d, w * S + z * 2 + yy), device_id_type=MESH,
        )

    def returns(z, act):
        for k in range(1, n_same):
            d, w = same(k)
            act(return_copy(z, d, w, zz, me_d, me_w))

        @pl.when(z != zz)
        def _():
            act(return_copy(z, me_d, me_w, zz, me_d, me_w))

    near = jnp.minimum(zz, Z - 1 - zz)

    def nth(m):
        alternating = ((m + 1) // 2) * (1 - 2 * (m % 2))
        far = m - near
        beyond = jnp.where(zz > Z - 1 - zz, -far, far)
        return zz + jnp.where(m <= 2 * near, alternating, beyond)

    def forward(z, h, act):
        @pl.when((z <= zz) & (zz + 1 < Z))
        def _():
            act(spread(z, yy, h, 0, (zz + 1, yy)))

        @pl.when((z >= zz) & (zz >= 1))
        def _():
            act(spread(z, yy, h, 1, (zz - 1, yy)))

        if h == 0:
            act(spread(z, yy, h, 2, (zz, 1 - yy)))
        else:

            @pl.when((z - zz != 1) & (zz - z != 1))
            def _():
                act(spread(z, yy, h, 2, (zz, 1 - yy)))

    def forward_other(act):
        @pl.when(zz + 1 < Z)
        def _():
            act(spread(zz, 1 - yy, 1, 3, (zz + 1, yy)))

        @pl.when(zz >= 1)
        def _():
            act(spread(zz, 1 - yy, 1, 4, (zz - 1, yy)))

    def start(copy):
        copy.start()

    def pass_on(k, h):
        @pl.when(zz - k >= 0)
        def _():
            spread(zz - k, yy, h, 2, (zz, 1 - yy)).wait_recv()
            forward(zz - k, h, start)

        @pl.when(zz + k < Z)
        def _():
            spread(zz + k, yy, h, 2, (zz, 1 - yy)).wait_recv()
            forward(zz + k, h, start)

    def arrive(m):
        z = nth(m)
        a_u = dh = 0.0
        for h in range(2):
            spread(z, 1 - yy, h, 2, (zz, 1 - yy)).wait_recv()
            if h == 1:

                @pl.when(m == 0)
                def _():
                    forward_other(start)

            both = buf[z, :, h].astype(F32).reshape(2 * n_dp * W, 2, CAP, half)
            x = both[:, 0].reshape(2 * rows, half).astype(BF16)
            g = both[:, 1].reshape(2 * rows, half).astype(BF16)
            cut = slice(h * half, (h + 1) * half)
            xall[z, :, cut] = x
            a_u = a_u + jnp.dot(x, gu_ref[cut], preferred_element_type=F32)
            dh = dh + jnp.dot(g, downt[cut], preferred_element_type=F32)
        a_u = a_u.reshape(2, n_dp, W * CAP, 2 * hidden)
        dh = dh.reshape(2, n_dp, W * CAP, hidden)
        part[z, :, :, : 2 * hidden] = jnp.concatenate([a_u[0], a_u[1]], axis=1).astype(BF16)
        part[z, :, :, 2 * hidden :] = jnp.concatenate([dh[0], dh[1]], axis=1).astype(BF16)
        for k in range(1, n_dp):
            reduce_copy(z, (me_d + k) % n_dp, me_d).start()

    def activate(m):
        z = nth(m)
        total = part[z, me_d].astype(F32)
        for k in range(1, n_dp):
            d = (me_d + k) % n_dp
            reduce_copy(z, d, d).wait_recv()
            total = total + prcv[z, d].astype(F32)
        pre = total[:, :hidden]
        up_part = total[:, hidden : 2 * hidden]
        dh = total[:, 2 * hidden :]
        sig = jax.nn.sigmoid(pre)
        dgate = dh * up_part * sig * (1.0 + pre * (1.0 - sig))
        dup = dh * (pre * sig)
        dgrcv[z, me_d] = jnp.concatenate(
            [dgate.reshape(2 * W, CAP, hidden), dup.reshape(2 * W, CAP, hidden)], axis=1
        ).astype(BF16)
        for k in range(1, n_dp):
            share_copy(z, (me_d + k) % n_dp, me_d).start()

    def give_back(m):
        z = nth(m)
        for k in range(1, n_dp):
            d = (me_d + k) % n_dp
            share_copy(z, d, d).wait_recv()
        both = dgrcv[z].astype(F32).reshape(n_dp, 2, W, 2, CAP, hidden)
        dgate = jnp.concatenate([both[:, y, :, 0].reshape(rows, hidden) for y in range(2)], axis=0)
        dup = jnp.concatenate([both[:, y, :, 1].reshape(rows, hidden) for y in range(2)], axis=0)
        dgu = jnp.concatenate([dgate, dup], axis=1).astype(BF16)
        dguall[z] = dgu
        dx = jnp.dot(dgu, gut[...], preferred_element_type=F32).astype(BF16)
        dxs[z] = dx.reshape(2, rows, cols)
        cross_copy(z).start()

    def combine(m):
        z = nth(m)
        cross_copy(z).wait_recv()
        both = dxs[z, yy].astype(F32) + across[z].astype(F32)
        both = both.reshape(n_dp, W, CAP, cols)
        sums[z] = jnp.concatenate([both[..., :half], both[..., half:]], axis=2).astype(BF16)
        returns(z, start)

    def step(m, carry):
        @pl.when(m < Z)
        def _():
            pass_on(m + 1, 1)
            arrive(m)
            pass_on(m + 2, 0)

        @pl.when((m >= 1) & (m < Z + 1))
        def _():
            activate(m - 1)

        @pl.when(m >= 2)
        def _():
            give_back(m - 2)

        @pl.when(m >= 3)
        def _():
            combine(m - 3)

        return carry

    for h in range(2):
        for k in range(1, n_same):
            pick_arrival(h, *same(k)).wait_recv()
        forward(zz, h, start)
    gu_in.wait()
    gut[...] = gu_ref[...].T
    pass_on(1, 0)
    lax.fori_loop(0, Z + 2, step, 0)

    def weight_gradient(h):
        cut = slice(h * half, (h + 1) * half)
        gw_ref[0, cut] = lax.dot_general(
            xall[:, :, cut].reshape(S * rows, half), dguall[...].reshape(S * rows, 2 * hidden), TN,
            preferred_element_type=F32,
        ).astype(BF16)

    def gradient_out(h):
        cut = pl.ds(h * half, half)
        return pltpu.make_async_copy(gw_ref.at[0, cut], gw_hbm.at[0, cut], s_out.at[h])

    weight_gradient(0)
    gradient_out(0).start()
    combine(Z - 1)
    weight_gradient(1)
    gradient_out(1).start()

    for k in range(1, n_same):
        for h in range(2):
            pick_copy(h, *same(k)).wait_send()

    def wait_send(copy):
        copy.wait_send()

    def drain(z, carry):
        for h in range(2):
            forward(z, h, wait_send)
        cross_copy(z).wait_send()
        for k in range(1, n_dp):
            d = (me_d + k) % n_dp
            reduce_copy(z, d, me_d).wait_send()
            share_copy(z, d, me_d).wait_send()
        returns(z, wait_send)
        return carry

    forward_other(wait_send)
    lax.fori_loop(0, Z, drain, 0)

    total = 0.0
    ret[zz, me_d, me_w] = sums[zz, me_d, me_w]
    for j in range(Z):
        z = (zz + j) % Z
        for k in range(1 if j == 0 else 0, n_same):
            d, w = same(k)
            return_copy(z, d, w, z, d, w).wait_recv()
        total = total + ret[z].astype(F32)
    fin_ref[...] = total.astype(BF16)
    gradient_out(0).wait()
    gradient_out(1).wait()


def place_rows(
    fin_hbm, slot_hbm, gw_in, gx_hbm, gw_hbm, fin_ref, slot_ref, gx_ref, gw_ref, s_in, s_out
):
    n_dp, W, _, half = fin_ref.shape
    tokens = gx_ref.shape[0]
    slot_copy = pltpu.make_async_copy(slot_hbm, slot_ref, s_in.at[0])
    fin_copy = pltpu.make_async_copy(fin_hbm, fin_ref, s_in.at[1])
    gw_copy = pltpu.make_async_copy(gw_in, gw_ref, s_in.at[2])
    for copy in (slot_copy, fin_copy, gw_copy):
        copy.start()
    gw_out = pltpu.make_async_copy(gw_ref, gw_hbm, s_in.at[3])
    outs = []
    slot_copy.wait()
    place = lax.broadcasted_iota(jnp.int32, (2 * CAP, tokens), 0)
    hits = []
    for h in range(2):
        for e in range(W):
            hit = (slot_ref[e : e + 1, :] == place - h * CAP) & (place >= h * CAP)
            hits.append(jnp.where(hit, 1.0, 0.0).T.astype(BF16))
    gw_copy.wait()
    gw_out.start()
    fin_copy.wait()
    for d in range(n_dp):
        for h in range(2):
            out = jnp.dot(hits[h * W], fin_ref[d, 0], preferred_element_type=F32)
            for e in range(1, W):
                out = out + jnp.dot(hits[h * W + e], fin_ref[d, e], preferred_element_type=F32)
            at = (2 * d + h) * half
            gx_ref[:, at : at + half] = out.astype(BF16)
        cut = pl.ds(2 * d * half, 2 * half)
        outs.append(pltpu.make_async_copy(gx_ref.at[:, cut], gx_hbm.at[:, cut], s_out.at[d]))
        outs[d].start()
    for copy in outs:
        copy.wait()
    gw_out.wait()


def on_device(n_dp, tokens, output_gradient, slot, gate_weight, gate_up_weight, down_weight):
    W = slot.shape[1]
    S = GROUP
    Z = S // 2
    _, cols, wide = gate_up_weight.shape
    hidden = wide // 2
    rows = n_dp * W * CAP
    vmem = pl.BlockSpec(memory_space=pltpu.VMEM)
    anywhere = pl.BlockSpec(memory_space=pl.ANY)
    dma = pltpu.SemaphoreType.DMA
    slot_row = slot.T
    fin, grad_gate_up = pl.pallas_call(
        functools.partial(kernel, n_dp, W),
        out_shape=(
            jax.ShapeDtypeStruct((n_dp, W, 2 * CAP, cols // 2), BF16),
            jax.ShapeDtypeStruct(gate_up_weight.shape, BF16),
        ),
        in_specs=[anywhere] * 6,
        out_specs=(vmem, anywhere),
        scratch_shapes=[
            pltpu.VMEM(tokens.shape, BF16),
            pltpu.VMEM(tokens.shape, BF16),
            pltpu.VMEM(slot_row.shape, jnp.int32),
            pltpu.VMEM(slot_row.shape, F32),
            pltpu.VMEM((cols, wide), BF16),
            pltpu.VMEM((hidden, cols), BF16),
            pltpu.VMEM((1, cols, wide), BF16),
            pltpu.VMEM((2, n_dp, W, 2 * CAP, cols // 2), BF16),
            pltpu.VMEM((Z, 2, 2, n_dp, W, 2 * CAP, cols // 2), BF16),
            pltpu.VMEM((Z, 2 * rows, cols), BF16),
            pltpu.VMEM((Z, n_dp, 2 * W * CAP, 3 * hidden), BF16),
            pltpu.VMEM((Z, n_dp, 2 * W * CAP, 3 * hidden), BF16),
            pltpu.VMEM((Z, n_dp, 2 * W, 2 * CAP, hidden), BF16),
            pltpu.VMEM((Z, 2 * rows, wide), BF16),
            pltpu.VMEM((Z, 2, rows, cols), BF16),
            pltpu.VMEM((Z, rows, cols), BF16),
            pltpu.VMEM((Z, n_dp, W, 2 * CAP, cols // 2), BF16),
            pltpu.VMEM((Z, n_dp, W, 2 * CAP, cols // 2), BF16),
            pltpu.VMEM((wide, cols), BF16),
            pltpu.VMEM((cols, hidden), BF16),
            dma((4 + 2 * n_dp,)), dma((2,)),
            dma((2, n_dp, W)), dma((2, n_dp, W)),
            dma((Z, 2, 5)), dma((Z, 2, 2)),
            dma((Z, n_dp)), dma((Z, n_dp)),
            dma((Z, n_dp)), dma((Z, n_dp)),
            dma((Z,)), dma((Z,)),
            dma((Z, n_dp, W)), dma((Z, n_dp, W)),
        ],
        compiler_params=pltpu.CompilerParams(
            collective_id=0, has_side_effects=True, vmem_limit_bytes=58 * 1024 * 1024
        ),
        cost_estimate=pl.CostEstimate(
            flops=14 * S * rows * cols * hidden,
            bytes_accessed=4 * tokens.size + 4 * gate_up_weight.size, transcendentals=0,
        ),
        name="routed_backward",
    )(tokens, output_gradient, slot_row, gate_weight.T, gate_up_weight[0], down_weight[0])
    return pl.pallas_call(
        place_rows,
        out_shape=(
            jax.ShapeDtypeStruct(tokens.shape, BF16),
            jax.ShapeDtypeStruct(gate_up_weight.shape, BF16),
        ),
        in_specs=[anywhere] * 3,
        out_specs=(anywhere, anywhere),
        scratch_shapes=[
            pltpu.VMEM(fin.shape, BF16),
            pltpu.VMEM(slot_row.shape, jnp.int32),
            pltpu.VMEM(tokens.shape, BF16),
            pltpu.VMEM(gate_up_weight.shape, BF16),
            dma((4,)), dma((n_dp,)),
        ],
        compiler_params=pltpu.CompilerParams(vmem_limit_bytes=58 * 1024 * 1024),
        name="place_rows",
    )(fin, slot_row, grad_gate_up)


def solution(mesh):
    in_specs = (
        P(("dp", "expert"), None),
        P(("dp", "expert"), None),
        P(("dp", "expert"), None),
        P(("dp", "expert"), None),
        P("expert", "dp", None),
        P("expert", None, "dp"),
    )
    out_specs = (P(("dp", "expert"), None), P("expert", "dp", None))
    return jax.shard_map(
        functools.partial(on_device, mesh.shape["dp"]),
        mesh=mesh, in_specs=in_specs, out_specs=out_specs, check_vma=False,
    )
```
